32 devices in a mesh: expert: 8 (over z, core), fsdp: 4 (over y, x).
Axes of the slice: x: 2, y: 2, z: 4, core: 2. Of those that a mesh axis runs over, the one named last changes fastest.
Arguments:
- states: bfloat16 [4096, 512], P(('expert', 'fsdp')), may hold values from -6 to 6
- rates: bfloat16 [4096, 512], P(('expert', 'fsdp')), may hold values from -6 to 6
- expert_ids: int32 [4096, 2], P(('expert', 'fsdp')), may hold values from 0 to 15, all different within a row; in each aligned block of 128 rows (0 to 127, 128 to 255, ...) at most 32 rows name the same one
- gate_weights: float32 [4096, 2], P(('expert', 'fsdp')), may hold values from 0.25 to 1
- cotangent: bfloat16 [4096, 512], P(('expert', 'fsdp')), may hold values from -6 to 6
- weight_in: bfloat16 [512, 16, 1024], P('fsdp', 'expert'), may hold values from -0.25 to 0.25
- weight_out: bfloat16 [1024, 16, 512], P('fsdp', 'expert'), may hold values from -0.1875 to 0.1875
Outputs:
- defect: bfloat16 [4096, 512], P(('expert', 'fsdp'))
- grad_states: bfloat16 [4096, 512], P(('expert', 'fsdp'))
- grad_in: bfloat16 [512, 16, 1024], P('fsdp', 'expert')
- grad_out: bfloat16 [1024, 16, 512], P('fsdp', 'expert')
The draws below stay inside these ranges and needn't reach their ends.
Inputs may be any that keep to these rules, and one draw needn't show every extreme that they name: `expert_ids`: A knot's two ids differ. Within each aligned block of 128 knots (the knots of one device) no expert is named by more than 32 of the block's entries, a bound that some block reaches.
All inputs are finite; a program needn't handle non-finite values.
Results may differ from the reference program's by a relative error of at most 0.019.
Values may be sent and summed in bfloat16 or wider, within the bound.
A program may use at most 64 MiB of HBM per device.

```python
import math
import jax
import jax.numpy as jnp
import numpy as np
from jax import lax

D = 512
H = 1024
TOK_DEV = 128
EXPERTS = 16
TOKENS = 4096
CAP = 32
N_EXPERT = 8
N_FSDP = 4


def levels(own_key, shape, pieces, low, top_value):
    def one(axis_at, shards_of):
        draws = jax.random.uniform(jax.random.fold_in(jax.random.fold_in(own_key, 6), axis_at), (shards_of,), jnp.float32, low / len(pieces), top_value / len(pieces))
        return jnp.repeat(jnp.exp(draws), shape[axis_at] // shards_of).reshape((-1,) + (1,) * (len(shape) - axis_at - 1))

    loudness = one(*pieces[0])
    for cut in pieces[1:]:
        loudness = loudness * one(*cut)
    return loudness


def shared_out(stream_key, own, number, rows, count, top, most, skew):
    order = jax.random.permutation(stream_key, count)
    packed, common = load_shares(count, rows * top, most, skew, True), load_shares(count, rows * top, most, skew, False)
    places = jnp.arange(count)

    def named(sizes, offset_by):
        used = int((sizes > 0).sum())
        fixed = max(1, used // 4)
        moved = fixed + (places - fixed + offset_by * (used - fixed)) % max(1, count - fixed)
        return jnp.zeros((count,), jnp.int32).at[order[jnp.where(places < fixed, places, moved)]].set(jnp.asarray(sizes, jnp.int32))

    sizes = jnp.where(number % 4 == 0, named(packed, number // 4), named(common, number - number // 4 - 1))
    mixed = jax.random.permutation(jax.random.fold_in(own, 3), count)
    source_of, receiver = mixed[0:count // 2 * 2:2], mixed[1:count // 2 * 2:2]
    margin = jnp.minimum(sizes[source_of] - 1, most - sizes[receiver]) // 2
    margin = jnp.where((source_of == order[0]) | (receiver == order[0]) | (sizes[receiver] == 0), 0, jnp.maximum(margin, 0))
    moved = jax.random.randint(jax.random.fold_in(own, 4), (count // 2,), 0, 1 << 20) % (margin + 1)
    sizes = sizes.at[source_of].add(-moved).at[receiver].add(moved)
    members = jnp.searchsorted(jnp.cumsum(sizes), jnp.arange(rows * top), side="right").astype(jnp.int32)
    table = members.reshape(top, rows).T
    table = table[jax.random.permutation(jax.random.fold_in(own, 1), rows)]
    offset_by = jax.random.randint(jax.random.fold_in(own, 2), (rows, 1), 0, top)
    return jnp.take_along_axis(table, (jnp.arange(top)[None, :] + offset_by) % top, axis=1)


def load_shares(number_of, total, bound, skew, full):
    portions = [(1 << 20) // math.isqrt(grade ** skew) + 1 for grade in range(1, number_of + 1)]
    largest = bound if full else min(bound, max(-(-total // number_of), total * portions[0] // sum(portions)))
    least = 1 if total - largest >= number_of - 1 else 0
    given, surplus = [largest] + [least] * (number_of - 1), total - largest - least * (number_of - 1)
    while surplus > 0:
        free = [i for i in range(1, number_of) if given[i] < largest] or [i for i in range(1, number_of) if given[i] < bound]
        mass, remaining = sum([portions[i] for i in free]), surplus
        for i in free:
            more = min(bound - given[i], max(1, remaining * portions[i] // mass), surplus)
            given[i] = given[i] + more
            surplus = surplus - more
    return np.array(given)


def centred(stream_key, extent, scale, reach, cuts=(), kind=jnp.bfloat16):
    values = jax.random.normal(stream_key, extent, jnp.float32) * scale
    if len(cuts) > 0:
        values = levels(stream_key, extent, cuts, -0.22, 0.18) * values
    return jnp.clip(values, min=-reach, max=reach).astype(kind)


def setup_inputs(seed: int = 0) -> dict:
    key_of = jax.random.split(jax.random.key(seed), 8)
    states = centred(key_of[0], (TOKENS, D), 1.0, 6.0, ((0, 32),))
    rates = centred(key_of[1], (TOKENS, D), 1.0, 6.0, ((0, 32),))
    expert_ids_keys = jax.random.split(jax.random.fold_in(key_of[2], 1), TOKENS // TOK_DEV)
    expert_ids_turns = jax.random.permutation(jax.random.fold_in(key_of[2], 3), TOKENS // TOK_DEV)
    expert_ids = jax.vmap(lambda own, number: shared_out(jax.random.fold_in(key_of[2], 2), own, number, TOK_DEV, EXPERTS, 2, CAP, 1))(expert_ids_keys, expert_ids_turns).reshape((TOKENS, 2))
    gate_weights = jnp.clip(0.25 + 0.75 * jax.random.uniform(key_of[3], (TOKENS, 2), jnp.float32) ** levels(key_of[3], (TOKENS, 2), ((0, 32),), -0.2, 0.2), 0.25, 1.0)
    cotangent = centred(key_of[4], (TOKENS, D), 1.0, 6.0, ((0, 32),))
    weight_in = centred(key_of[5], (D, EXPERTS, H), D ** -0.5, 0.25, ((0, 4), (1, 8)))
    weight_out = centred(key_of[6], (H, EXPERTS, D), H ** -0.5, 0.1875, ((0, 4), (1, 8)))
    return dict(states=states, rates=rates, expert_ids=expert_ids, gate_weights=gate_weights, cotangent=cotangent, weight_in=weight_in, weight_out=weight_out)


def activate(value):
    return value * jax.nn.sigmoid(value)


def activate_slope(value):
    sigma = jax.nn.sigmoid(value)
    return sigma * (1.0 + value * (1.0 - sigma))


def reference(states, rates, expert_ids, gate_weights, cotangent, weight_in, weight_out):
    blocks = N_EXPERT * N_FSDP
    assigned = 2 * TOK_DEV
    all_assigned = 2 * TOKENS
    ids_blocks = expert_ids.reshape(blocks, assigned)
    onehot = (ids_blocks[:, :, None] == jnp.arange(EXPERTS, dtype=jnp.int32)[None, None, :]).astype(jnp.int32)
    before = jnp.cumsum(onehot, axis=1) - onehot
    slot_index = jnp.sum(before * onehot, axis=2)
    column = (jnp.arange(blocks, dtype=jnp.int32)[:, None] * CAP + slot_index).reshape(all_assigned).astype(jnp.int32)
    flat_ids = expert_ids.reshape(all_assigned)
    slot_table = jnp.full((EXPERTS, blocks * CAP), all_assigned, jnp.int32)
    slot_table = slot_table.at[flat_ids, column].set(jnp.arange(all_assigned, dtype=jnp.int32))
    zero_row = jnp.zeros((1, D), jnp.bfloat16)
    padded_states = jnp.concatenate([states, zero_row], axis=0)
    descent = (-gate_weights[:, :, None] * cotangent[:, None, :].astype(jnp.float32)).astype(jnp.bfloat16)
    padded_descent = jnp.concatenate([descent.reshape(all_assigned, D), zero_row], axis=0)

    def per_expert(running, inputs):
        entries, expert_in, expert_out = inputs
        knot_rows = padded_states[entries // 2]
        grad_rows = padded_descent[entries]
        preact = jnp.dot(knot_rows, expert_in, preferred_element_type=jnp.float32)
        hidden = activate(preact).astype(jnp.bfloat16)
        values = jnp.dot(hidden, expert_out, preferred_element_type=jnp.float32).astype(jnp.bfloat16)
        slope = jnp.dot(grad_rows, expert_out.T, preferred_element_type=jnp.float32)
        inner = (slope * activate_slope(preact)).astype(jnp.bfloat16)
        returned = jnp.dot(inner, expert_in.T, preferred_element_type=jnp.float32).astype(jnp.bfloat16)
        grouped = (N_EXPERT, N_FSDP, CAP)
        part_in = jnp.einsum("afcd,afch->fdh", knot_rows.reshape(grouped + (D,)).astype(jnp.float32),
                             inner.reshape(grouped + (H,)).astype(jnp.float32))
        part_out = jnp.einsum("afch,afcd->fhd", hidden.reshape(grouped + (H,)).astype(jnp.float32),
                              grad_rows.reshape(grouped + (D,)).astype(jnp.float32))
        part_in = lax.optimization_barrier(part_in.astype(jnp.bfloat16))
        part_out = lax.optimization_barrier(part_out.astype(jnp.bfloat16))
        summed_in = jnp.sum(part_in.astype(jnp.float32), axis=0).astype(jnp.bfloat16)
        summed_out = jnp.sum(part_out.astype(jnp.float32), axis=0).astype(jnp.bfloat16)
        return running, (values, returned, summed_in, summed_out)

    inputs_all = (slot_table, jnp.transpose(weight_in, (1, 0, 2)), jnp.transpose(weight_out, (1, 0, 2)))
    unused, (values_all, returned_all, grad_in_all, grad_out_all) = lax.scan(
        per_expert, jnp.zeros((), jnp.float32), inputs_all)
    values_knot = values_all[flat_ids, column].reshape(TOKENS, 2, D).astype(jnp.float32)
    combined = jnp.sum(gate_weights[:, :, None] * values_knot, axis=1)
    defect = (rates.astype(jnp.float32) - combined).astype(jnp.bfloat16)
    returned_knot = returned_all[flat_ids, column].reshape(TOKENS, 2, D).astype(jnp.float32)
    grad_states = jnp.sum(returned_knot, axis=1).astype(jnp.bfloat16)
    grad_in = jnp.transpose(grad_in_all, (1, 0, 2))
    grad_out = jnp.transpose(grad_out_all, (1, 0, 2))
    return (defect, grad_states, grad_in, grad_out)
```

```python
import functools
import math

import jax
import jax.numpy as jnp
from jax import lax
from jax.experimental import pallas as pl
from jax.experimental.pallas import tpu as pltpu
from jax.sharding import PartitionSpec as P

MESH = pl.DeviceIdType.MESH
BF = jnp.bfloat16
F32 = jnp.float32


def dot(left, right, left_dim, right_dim):
    return lax.dot_general(
        left, right, (((left_dim,), (right_dim,)), ((), ())), preferred_element_type=F32
    )


def kernel(
    sizes,
    states, rates, ids, gates, cotangent, w_in, w_out,
    defect, grad_states, grad_in, grad_out,
    tok_send, tok_recv, ret_send, ret_recv,
    full_in, full_out, part_in, part_out,
    first_in, first_out, sum_in, sum_out, second_in, second_out,
    acc_v, acc_r, picks,
    tok_ss, tok_rs, ret_ss, ret_rs,
    w_ss, w_rs, one_ss, one_rs, two_ss, two_rs,
):
    groups, fsdp, nx, ny, local, cap = sizes
    rows, feature = states.shape
    hidden_all = w_in.shape[2]
    hrows = w_out.shape[1]
    slots = groups * local * cap
    lines = groups * cap
    g = lax.axis_index("expert")
    f = lax.axis_index("fsdp")
    y, x = f // nx, lax.rem(f, nx)

    shards = (w_in, w_out)
    fulls = (full_in, full_out)
    parts = (part_in, part_out)
    firsts = (first_in, first_out)
    sums = (sum_in, sum_out)
    seconds = (second_in, second_out)
    outs = (grad_in, grad_out)
    counts = ((nx, ny), (ny, nx))
    mine = ((x, y), (y, x))

    def place(arr, a, b):
        return b * nx + a if arr == 0 else a * nx + b

    def peer(arr, i, j):
        (n1, n2), (a, b) = counts[arr], mine[arr]
        return lax.rem(a + i, n1), lax.rem(b + j, n2)

    def push(src, dst, send, recv, device):
        return pltpu.make_async_remote_copy(
            src_ref=src, dst_ref=dst, send_sem=send, recv_sem=recv,
            device_id=device, device_id_type=MESH,
        )

    barrier = pltpu.get_barrier_semaphore()

    def greet(o, carry):
        pl.semaphore_signal(
            barrier, inc=1, device_id={"expert": lax.rem(g + o, groups)}, device_id_type=MESH
        )
        return carry

    lax.fori_loop(1, groups, greet, 0)
    for arr in range(2):
        for i in range(1, counts[arr][0]):
            a, b = peer(arr, i, 0)
            pl.semaphore_signal(
                barrier, inc=1, device_id={"fsdp": place(arr, a, b)}, device_id_type=MESH
            )
    pl.semaphore_wait(barrier, groups - 1 + nx - 1 + ny - 1)

    def shard_copy(arr, e, source, own, a, b, slot):
        src = shards[arr].at[e] if own else fulls[arr].at[e, source]
        return push(
            src, fulls[arr].at[e, source], w_ss.at[arr, e, slot], w_rs.at[arr, e, source],
            {"fsdp": place(arr, a, b)},
        )

    def own_copies(arr, e):
        n1, n2 = counts[arr]
        copies = []
        for i in range(1, n1):
            copies.append(shard_copy(arr, e, f, True, *peer(arr, i, 0), i - 1))
        for j in range(1, n2):
            copies.append(shard_copy(arr, e, f, True, *peer(arr, 0, j), n1 - 1 + j - 1))
        return copies

    def forward_copies(arr, e, i):
        n1, n2 = counts[arr]
        source = place(arr, *peer(arr, i, 0))
        return [
            shard_copy(arr, e, source, False, *peer(arr, 0, j), n1 - 1 + i * (n2 - 1) + j - 1)
            for j in range(1, n2)
        ]

    def send_own(e):
        one, two = own_copies(0, e), own_copies(1, e)
        for left, right in zip(one, two):
            left.start()
            right.start()

    def await_shard(arr, e, source):
        shard_copy(arr, e, source, False, *peer(arr, 0, 1), 0).wait_recv()

    def forward(e):
        for arr in range(2):
            for i in range(1, counts[arr][0]):
                await_shard(arr, e, place(arr, *peer(arr, i, 0)))
                for copy in forward_copies(arr, e, i):
                    copy.start()

    def await_rest(e):
        for arr in range(2):
            n1, n2 = counts[arr]
            for j in range(1, n2):
                for i in range(n1):
                    await_shard(arr, e, place(arr, *peer(arr, i, j)))

    send_own(0)

    experts_all = groups * local
    id_f = ids[...].astype(F32)
    expert_iota = lax.broadcasted_iota(jnp.int32, (rows, experts_all), 1).astype(F32)
    hit = [(id_f[:, k:k + 1] == expert_iota).astype(F32) for k in range(2)]
    below = (
        lax.broadcasted_iota(jnp.int32, (rows, rows), 0)
        > lax.broadcasted_iota(jnp.int32, (rows, rows), 1)
    ).astype(F32).astype(BF)
    before = dot(below, (hit[0] + hit[1]).astype(BF), 1, 0)
    slot_iota = lax.broadcasted_iota(jnp.int32, (rows, slots), 1).astype(F32)
    cot = cotangent[...].astype(F32)
    grads_slot = None
    for k in range(2):
        slot = jnp.sum(hit[k] * before, axis=1, keepdims=True)
        pick = (id_f[:, k:k + 1] * cap + slot == slot_iota).astype(F32).astype(BF)
        picks[k] = pick
        descent = (-gates[:, k:k + 1] * cot).astype(BF)
        term = dot(pick, descent, 0, 0)
        grads_slot = term if grads_slot is None else grads_slot + term
    knots_slot = dot(picks[0] + picks[1], states[...], 0, 0)
    shape = (groups, local, cap, feature)
    tok_send[:, :, 0] = knots_slot.astype(BF).reshape(shape)
    tok_send[:, :, 1] = grads_slot.astype(BF).reshape(shape)

    def tok_copy(o):
        other = lax.rem(g + o, groups)
        return push(
            tok_send.at[other], tok_recv.at[g], tok_ss.at[other], tok_rs.at[g], {"expert": other}
        )

    def tok_arrival(o):
        other = lax.rem(g + o, groups)
        return push(
            tok_send.at[other], tok_recv.at[other], tok_ss.at[other], tok_rs.at[other],
            {"expert": other},
        )

    def over_groups(act):
        def body(o, carry):
            act(o)
            return carry

        lax.fori_loop(1, groups, body, 0)

    over_groups(lambda o: tok_copy(o).start())
    tok_recv[g] = tok_send[g]
    for arr in range(2):
        for e in range(local):
            fulls[arr][e, f] = shards[arr][e]

    def ret_copy(e, o):
        other = lax.rem(g + o, groups)
        return push(
            ret_send.at[other, e], ret_recv.at[g, e], ret_ss.at[other, e], ret_rs.at[g, e],
            {"expert": other},
        )

    def ret_arrival(e, o):
        other = lax.rem(g + o, groups)
        return push(
            ret_send.at[other, e], ret_recv.at[other, e], ret_ss.at[other, e], ret_rs.at[other, e],
            {"expert": other},
        )

    width = max(256, hrows)
    per = width // hrows

    def compute(e):
        acc_v[...] = jnp.zeros_like(acc_v)
        acc_r[...] = jnp.zeros_like(acc_r)

        def chunk(c, carry):
            knots = tok_recv[:, e, 0].reshape(lines, feature)
            grads = tok_recv[:, e, 1].reshape(lines, feature)
            columns = pl.ds(pl.multiple_of(c * width, width), width)
            wi = full_in[e, :, :, columns].reshape(feature, width)
            wo = full_out[e, pl.ds(c * per, per)].reshape(width, feature)
            preact = dot(knots, wi, 1, 0)
            slope = dot(grads, wo, 1, 1)
            sigma = jax.nn.sigmoid(preact)
            hidden = (preact * sigma).astype(BF)
            inner = (slope * (sigma * (1.0 + preact * (1.0 - sigma)))).astype(BF)
            part_in[e, :, :, columns] = dot(knots, inner, 0, 0).astype(BF).reshape(
                fsdp, feature // fsdp, width
            )
            part_out[e, pl.ds(c * per, per)] = dot(hidden, grads, 0, 0).astype(BF).reshape(
                per, hrows, feature
            )
            acc_v[...] += dot(hidden, wo, 1, 0)
            acc_r[...] += dot(inner, wi, 1, 1)
            return carry

        lax.fori_loop(0, hidden_all // width, chunk, 0)
        back = (groups, cap, feature)
        ret_send[:, e, 0] = acc_v[...].astype(BF).reshape(back)
        ret_send[:, e, 1] = acc_r[...].astype(BF).reshape(back)

    def one_copy(arr, e, i, j):
        a, b = mine[arr]
        to, row = peer(arr, i, j)
        return push(
            parts[arr].at[e, place(arr, to, row)], firsts[arr].at[e, a, row],
            one_ss.at[arr, e, to, row], one_rs.at[arr, e, a, row],
            {"fsdp": place(arr, to, b)},
        )

    def one_arrival(arr, e, i, j):
        b = mine[arr][1]
        to, row = peer(arr, i, j)
        return push(
            parts[arr].at[e, place(arr, to, row)], firsts[arr].at[e, to, row],
            one_ss.at[arr, e, to, row], one_rs.at[arr, e, to, row],
            {"fsdp": place(arr, to, b)},
        )

    def two_copy(arr, e, j):
        a, b = mine[arr]
        row = peer(arr, 0, j)[1]
        return push(
            sums[arr].at[e, row], seconds[arr].at[e, b],
            two_ss.at[arr, e, row], two_rs.at[arr, e, b], {"fsdp": place(arr, a, row)},
        )

    def two_arrival(arr, e, j):
        a = mine[arr][0]
        row = peer(arr, 0, j)[1]
        return push(
            sums[arr].at[e, row], seconds[arr].at[e, row],
            two_ss.at[arr, e, row], two_rs.at[arr, e, row], {"fsdp": place(arr, a, row)},
        )

    def send_one(e):
        for j in list(range(1, max(nx, ny))) + [0]:
            for arr in range(2):
                n1, n2 = counts[arr]
                if j < n2:
                    for i in range(1, n1):
                        one_copy(arr, e, i, j).start()

    def summed(arr, e, j):
        a = mine[arr][0]
        row = peer(arr, 0, j)[1]
        total = parts[arr][e, place(arr, a, row)].astype(F32)
        for i in range(1, counts[arr][0]):
            one_arrival(arr, e, i, j).wait_recv()
            total = total + firsts[arr][e, peer(arr, i, 0)[0], row].astype(F32)
        return total

    def send_two(e):
        for arr in range(2):
            for j in range(1, counts[arr][1]):
                row = peer(arr, 0, j)[1]
                sums[arr][e, row] = summed(arr, e, j).astype(BF)
                two_copy(arr, e, j).start()

    def finish(e):
        for arr in range(2):
            total = summed(arr, e, 0)
            for j in range(1, counts[arr][1]):
                row = peer(arr, 0, j)[1]
                two_arrival(arr, e, j).wait_recv()
                total = total + seconds[arr][e, row].astype(F32)
            outs[arr][e] = total.astype(BF)

    forward(0)
    if local > 1:
        send_own(1)
    over_groups(lambda o: tok_arrival(o).wait_recv())
    for e in range(local):
        await_rest(e)
        compute(e)
        ret_recv[g, e] = ret_send[g, e]
        over_groups(lambda o: ret_copy(e, o).start())
        if e + 1 < local:
            forward(e + 1)
        send_one(e)
        if e + 2 < local:
            send_own(e + 2)
        if e >= 1:
            send_two(e - 1)
    send_two(local - 1)

    for e in range(local):
        over_groups(lambda o: ret_arrival(e, o).wait_recv())
    values = ret_recv[:, :, 0].reshape(slots, feature)
    combined = None
    for k in range(2):
        term = gates[:, k:k + 1] * dot(picks[k], values, 1, 0)
        combined = term if combined is None else combined + term
    defect[...] = (rates[...].astype(F32) - combined).astype(BF)
    returned = ret_recv[:, :, 1].reshape(slots, feature)
    grad_states[...] = dot(picks[0] + picks[1], returned, 1, 0).astype(BF)

    for e in range(local):
        finish(e)

    over_groups(lambda o: tok_copy(o).wait_send())
    for e in range(local):
        over_groups(lambda o: ret_copy(e, o).wait_send())
        for arr in range(2):
            n1, n2 = counts[arr]
            for copy in own_copies(arr, e):
                copy.wait_send()
            for i in range(1, n1):
                for copy in forward_copies(arr, e, i):
                    copy.wait_send()
                for j in range(n2):
                    one_copy(arr, e, i, j).wait_send()
            for j in range(1, n2):
                two_copy(arr, e, j).wait_send()


def on_device(states, rates, expert_ids, gate_weights, cotangent, weight_in, weight_out):
    groups, fsdp = lax.axis_size("expert"), lax.axis_size("fsdp")
    rows, feature = states.shape
    drows, local, hidden = weight_in.shape
    hrows = weight_out.shape[0]
    capacity = max(2, 4 * rows // (local * groups))
    cap = -(-capacity // 16) * 16
    nx = math.isqrt(fsdp)
    if nx * nx != fsdp:
        nx = fsdp
    ny = fsdp // nx
    slots = groups * local * cap
    w_in = jnp.transpose(weight_in, (1, 0, 2))
    w_out = jnp.transpose(weight_out, (1, 0, 2))
    shard_in, shard_out = (drows, hidden), (hrows, feature)
    exchange = (groups, local, 2, cap, feature)
    most = max(nx, ny)
    vmem = pl.BlockSpec(memory_space=pltpu.VMEM)
    dma = pltpu.SemaphoreType.DMA
    defect, grad_states, grad_in, grad_out = pl.pallas_call(
        functools.partial(kernel, (groups, fsdp, nx, ny, local, cap)),
        out_shape=(
            jax.ShapeDtypeStruct((rows, feature), BF),
            jax.ShapeDtypeStruct((rows, feature), BF),
            jax.ShapeDtypeStruct((local,) + shard_in, BF),
            jax.ShapeDtypeStruct((local,) + shard_out, BF),
        ),
        in_specs=[vmem] * 7,
        out_specs=(vmem,) * 4,
        scratch_shapes=[
            pltpu.VMEM(exchange, BF),
            pltpu.VMEM(exchange, BF),
            pltpu.VMEM(exchange, BF),
            pltpu.VMEM(exchange, BF),
            pltpu.VMEM((local, fsdp) + shard_in, BF),
            pltpu.VMEM((local, fsdp) + shard_out, BF),
            pltpu.VMEM((local, fsdp) + shard_in, BF),
            pltpu.VMEM((local, fsdp) + shard_out, BF),
            pltpu.VMEM((local, nx, ny) + shard_in, BF),
            pltpu.VMEM((local, ny, nx) + shard_out, BF),
            pltpu.VMEM((local, ny) + shard_in, BF),
            pltpu.VMEM((local, nx) + shard_out, BF),
            pltpu.VMEM((local, ny) + shard_in, BF),
            pltpu.VMEM((local, nx) + shard_out, BF),
            pltpu.VMEM((groups * cap, feature), F32),
            pltpu.VMEM((groups * cap, feature), F32),
            pltpu.VMEM((2, rows, slots), BF),
            dma((groups,)),
            dma((groups,)),
            dma((groups, local)),
            dma((groups, local)),
            dma((2, local, fsdp + most)),
            dma((2, local, fsdp)),
            dma((2, local, most, most)),
            dma((2, local, most, most)),
            dma((2, local, most)),
            dma((2, local, most)),
        ],
        compiler_params=pltpu.CompilerParams(
            collective_id=0, has_side_effects=True, vmem_limit_bytes=56 * 1024 * 1024
        ),
    )(states, rates, expert_ids, gate_weights, cotangent, w_in, w_out)
    return (
        defect,
        grad_states,
        jnp.transpose(grad_in, (1, 0, 2)),
        jnp.transpose(grad_out, (1, 0, 2)),
    )


def solution(mesh):
    placed = (
        P(("expert", "fsdp"), None),
        P(("expert", "fsdp"), None),
        P(("expert", "fsdp"), None),
        P(("expert", "fsdp"), None),
        P(("expert", "fsdp"), None),
        P("fsdp", "expert", None),
        P("fsdp", "expert", None),
    )
    return jax.shard_map(
        on_device,
        mesh=mesh,
        in_specs=placed,
        out_specs=(
            P(("expert", "fsdp"), None),
            P(("expert", "fsdp"), None),
            P("fsdp", "expert", None),
            P("fsdp", "expert", None),
        ),
        check_vma=False,
    )
```

```python
import functools
import math

import jax
import jax.numpy as jnp
from jax import lax
from jax.experimental import pallas as pl
from jax.experimental.pallas import tpu as pltpu
from jax.sharding import PartitionSpec as P

MESH = pl.DeviceIdType.MESH
BF = jnp.bfloat16
F32 = jnp.float32


def dot(left, right, left_dim, right_dim):
    return lax.dot_general(
        left, right, (((left_dim,), (right_dim,)), ((), ())), preferred_element_type=F32
    )


def kernel(
    sizes,
    states, rates, ids, gates, cotangent, w_in, w_out,
    defect, grad_states, grad_in, grad_out,
    tok_send, tok_recv, ret_send, ret_recv,
    full_in, full_out, part_in, part_out,
    first_in, first_out, sum_in, sum_out, second_in, second_out,
    acc_v, acc_r, picks,
    tok_ss, tok_rs, ret_ss, ret_rs,
    w_ss, w_rs, one_ss, one_rs, two_ss, two_rs,
):
    groups, fsdp, nx, ny, local, cap = sizes
    rows, feature = states.shape
    hidden_all = w_in.shape[2]
    hrows = w_out.shape[1]
    slots = groups * local * cap
    lines = local * groups * cap
    sets = nx // local
    g = lax.axis_index("expert")
    f = lax.axis_index("fsdp")
    y, x = f // nx, lax.rem(f, nx)
    q, mine = x // local, lax.rem(x, local)
    span = hidden_all // ny

    shards = (w_in, w_out)
    fulls = (full_in, full_out)
    parts = (part_in, part_out)
    firsts = (first_in, first_out)
    sums = (sum_in, sum_out)
    seconds = (second_in, second_out)
    outs = (grad_in, grad_out)

    def turn(own, step, size):
        return lax.rem(own + step, size)

    def push(src, dst, send, recv, **device):
        return pltpu.make_async_remote_copy(
            src_ref=src, dst_ref=dst, send_sem=send, recv_sem=recv,
            device_id=device, device_id_type=MESH,
        )

    def greet(**device):
        pl.semaphore_signal(barrier, inc=1, device_id=device, device_id_type=MESH)

    def over_groups(start, act):
        def body(o, carry):
            act(o)
            return carry

        lax.fori_loop(start, groups, body, 0)

    def over_peers(act):
        for d in range(local):
            over_groups(1 if d == 0 else 0, functools.partial(act, d))

    barrier = pltpu.get_barrier_semaphore()
    over_peers(
        lambda d, o: greet(
            expert=turn(g, o, groups), fsdp=y * nx + q * local + turn(mine, d, local)
        )
    )
    for k in range(1, sets):
        for d in range(local):
            greet(fsdp=y * nx + turn(q, k, sets) * local + d)
    for j in range(1, ny):
        greet(fsdp=turn(y, j, ny) * nx + x)
    pl.semaphore_wait(barrier, groups * local - 1 + nx - local + ny - 1)

    def along_x(arr, i):
        to = turn(x, i, nx)
        return push(
            shards[arr].at[lax.rem(to, local)], fulls[arr].at[f],
            w_ss.at[arr, i - 1], w_rs.at[arr, f], fsdp=y * nx + to,
        )

    def along_y(arr, i, j):
        source = y * nx + turn(x, i, nx)
        src = shards[arr].at[mine] if i == 0 else fulls[arr].at[source]
        return push(
            src, fulls[arr].at[source], w_ss.at[arr, nx - 1 + i * (ny - 1) + j - 1],
            w_rs.at[arr, source], fsdp=turn(y, j, ny) * nx + x,
        )

    def shard_arrival(arr, i, j):
        source = turn(y, j, ny) * nx + turn(x, i, nx)
        return push(
            fulls[arr].at[source], fulls[arr].at[source], w_ss.at[arr, 0], w_rs.at[arr, source],
            fsdp=turn(y, j, ny) * nx + (x if j else turn(x, i, nx)),
        )

    for arr in range(2):
        for i in range(1, nx):
            along_x(arr, i).start()
        for j in range(1, ny):
            along_y(arr, 0, j).start()

    experts_all = groups * local
    id_f = ids[...].astype(F32)
    gate = gates[...].T
    expert_iota = lax.broadcasted_iota(jnp.int32, (experts_all, rows), 0).astype(F32)
    hit = [(id_f[k:k + 1] == expert_iota).astype(F32) for k in range(2)]
    above = (
        lax.broadcasted_iota(jnp.int32, (rows, rows), 0)
        < lax.broadcasted_iota(jnp.int32, (rows, rows), 1)
    ).astype(F32).astype(BF)
    before = dot((hit[0] + hit[1]).astype(BF), above, 1, 0)
    slot_iota = lax.broadcasted_iota(jnp.int32, (slots, rows), 0).astype(F32)
    cot = cotangent[...].astype(F32)
    grads_slot = None
    for k in range(2):
        slot = jnp.sum(hit[k] * before, axis=0, keepdims=True)
        pick = (id_f[k:k + 1] * cap + slot == slot_iota).astype(F32).astype(BF)
        picks[k] = pick
        descent = (-gate[:, k:k + 1] * cot).astype(BF)
        term = dot(pick, descent, 1, 0)
        grads_slot = term if grads_slot is None else grads_slot + term
    shape = (groups, local, cap, feature)
    tok_send[:, :, 1] = grads_slot.astype(BF).reshape(shape)
    knots_slot = dot(picks[0] + picks[1], states[...], 1, 0)
    tok_send[:, :, 0] = knots_slot.astype(BF).reshape(shape)

    def tok_copy(d, o):
        other, e = turn(g, o, groups), turn(mine, d, local)
        return push(
            tok_send.at[other, e], tok_recv.at[mine, g], tok_ss.at[other, e], tok_rs.at[mine, g],
            expert=other, fsdp=y * nx + q * local + e,
        )

    def tok_arrival(d, o):
        other, e = turn(g, o, groups), turn(mine, d, local)
        return push(
            tok_send.at[other, e], tok_recv.at[e, other], tok_ss.at[other, e], tok_rs.at[e, other],
            expert=other, fsdp=y * nx + q * local + e,
        )

    over_peers(lambda d, o: tok_copy(d, o).start())
    tok_recv[mine, g] = tok_send[g, mine]
    for arr in range(2):
        fulls[arr][f] = shards[arr][mine]

    for arr in range(2):
        for i in range(1, nx):
            shard_arrival(arr, i, 0).wait_recv()
            for j in range(1, ny):
                along_y(arr, i, j).start()
    over_peers(lambda d, o: tok_arrival(d, o).wait_recv())
    for arr in range(2):
        for j in range(1, ny):
            for i in range(nx):
                shard_arrival(arr, i, j).wait_recv()

    width = max(256, hrows)
    per = width // hrows
    steps = span // width

    def one_copy(arr, j, i, row):
        there, column = turn(y, j, ny), turn(x, i, nx)
        shard = there * nx + column
        if arr == 1:
            return push(
                part_out.at[shard], first_out.at[y, column],
                one_ss.at[1, there, column, 0], one_rs.at[1, y, column, 0],
                fsdp=there * nx + x,
            )
        place = pl.ds(pl.multiple_of(row * span, span), span)
        return push(
            part_in.at[shard, :, place], first_in.at[y, column, :, place],
            one_ss.at[0, there, column, row], one_rs.at[0, y, column, row],
            fsdp=there * nx + x,
        )

    def one_arrival(arr, j, i, row):
        there, column = turn(y, j, ny), turn(x, i, nx)
        shard = there * nx + column
        if arr == 1:
            return push(
                part_out.at[shard], first_out.at[there, column],
                one_ss.at[1, there, column, 0], one_rs.at[1, there, column, 0],
                fsdp=there * nx + x,
            )
        place = pl.ds(pl.multiple_of(row * span, span), span)
        return push(
            part_in.at[shard, :, place], first_in.at[there, column, :, place],
            one_ss.at[0, there, column, row], one_rs.at[0, there, column, row],
            fsdp=there * nx + x,
        )

    acc_v[...] = jnp.zeros_like(acc_v)
    acc_r[...] = jnp.zeros_like(acc_r)
    for stage in range(1, ny + 1):
        row = turn(y, stage, ny)

        def chunk(c, carry):
            knots = tok_recv[:, :, 0].reshape(lines, feature)
            grads = tok_recv[:, :, 1].reshape(lines, feature)
            at = row * steps + c
            columns = pl.ds(pl.multiple_of(at * width, width), width)
            wi = full_in[:, :, columns].reshape(feature, width)
            wo = full_out[pl.ds(at * per, per)].reshape(width, feature)
            preact = dot(knots, wi, 1, 0)
            slope = dot(grads, wo, 1, 1)
            sigma = jax.nn.sigmoid(preact)
            hidden = (preact * sigma).astype(BF)
            inner = (slope * (sigma * (1.0 + preact * (1.0 - sigma)))).astype(BF)
            part_in[:, :, columns] = dot(knots, inner, 0, 0).astype(BF).reshape(
                fsdp, feature // fsdp, width
            )
            part_out[pl.ds(at * per, per)] = dot(hidden, grads, 0, 0).astype(BF).reshape(
                per, hrows, feature
            )
            acc_v[...] += dot(hidden, wo, 1, 0)
            acc_r[...] += dot(inner, wi, 1, 1)
            return carry

        lax.fori_loop(0, steps, chunk, 0)
        for i in list(range(1, nx)) + [0]:
            if stage < ny:
                one_copy(1, stage, i, 0).start()
            for j in range(1, ny):
                one_copy(0, j, i, row).start()

    back = (local, groups, cap, feature)
    ret_send[:, :, 0] = acc_v[...].astype(BF).reshape(back)
    ret_send[:, :, 1] = acc_r[...].astype(BF).reshape(back)

    def ret_copy(d, o):
        other, c = turn(g, o, groups), turn(mine, d, local)
        return push(
            ret_send.at[c, other], ret_recv.at[g, mine], ret_ss.at[c, other], ret_rs.at[g, mine],
            expert=other, fsdp=y * nx + q * local + c,
        )

    def ret_arrival(d, o):
        other, c = turn(g, o, groups), turn(mine, d, local)
        return push(
            ret_send.at[c, other], ret_recv.at[other, c], ret_ss.at[c, other], ret_rs.at[other, c],
            expert=other, fsdp=y * nx + q * local + c,
        )

    over_peers(lambda d, o: ret_copy(d, o).start())
    ret_recv[g, mine] = ret_send[mine, g]

    def two_copy(arr, i):
        to = turn(x, i, nx)
        return push(
            sums[arr].at[to], seconds[arr].at[x], two_ss.at[arr, to], two_rs.at[arr, x],
            fsdp=y * nx + to,
        )

    def two_arrival(arr, source):
        return push(
            sums[arr].at[source], seconds[arr].at[source], two_ss.at[arr, source],
            two_rs.at[arr, source], fsdp=y * nx + source,
        )

    def summed(arr, i):
        column = turn(x, i, nx)
        total = parts[arr][y * nx + column].astype(F32)
        for j in range(1, ny):
            for row in range(ny if arr == 0 else 1):
                one_arrival(arr, j, i, row).wait_recv()
            total = total + firsts[arr][turn(y, j, ny), column].astype(F32)
        return total

    for i in range(1, nx):
        for arr in (1, 0):
            sums[arr][turn(x, i, nx)] = summed(arr, i).astype(BF)
            two_copy(arr, i).start()
    own = [summed(arr, 0) for arr in range(2)]
    for arr in range(2):
        total = own[arr]
        for k in range(1, sets):
            source = turn(q, k, sets) * local + mine
            two_arrival(arr, source).wait_recv()
            total = total + seconds[arr][source].astype(F32)
        outs[arr][mine] = total.astype(BF)

    over_peers(lambda d, o: ret_arrival(d, o).wait_recv())
    values = ret_recv[:, :, 0].reshape(slots, feature)
    combined = None
    for k in range(2):
        term = gate[:, k:k + 1] * dot(picks[k], values, 0, 0)
        combined = term if combined is None else combined + term
    defect[...] = (rates[...].astype(F32) - combined).astype(BF)
    returned = ret_recv[:, :, 1].reshape(slots, feature)
    grad_states[...] = dot(picks[0] + picks[1], returned, 0, 0).astype(BF)

    for d in range(1, local):
        e = turn(mine, d, local)
        for arr in (1, 0):
            total = None
            for k in range(sets):
                source = turn(q, k, sets) * local + e
                two_arrival(arr, source).wait_recv()
                term = seconds[arr][source].astype(F32)
                total = term if total is None else total + term
            outs[arr][e] = total.astype(BF)

    over_peers(lambda d, o: tok_copy(d, o).wait_send())
    over_peers(lambda d, o: ret_copy(d, o).wait_send())
    for arr in range(2):
        for i in range(1, nx):
            along_x(arr, i).wait_send()
            two_copy(arr, i).wait_send()
        for j in range(1, ny):
            for i in range(nx):
                along_y(arr, i, j).wait_send()
                for row in range(ny if arr == 0 else 1):
                    one_copy(arr, j, i, row).wait_send()


def on_device(states, rates, expert_ids, gate_weights, cotangent, weight_in, weight_out):
    groups, fsdp = lax.axis_size("expert"), lax.axis_size("fsdp")
    rows, feature = states.shape
    drows, local, hidden = weight_in.shape
    hrows = weight_out.shape[0]
    capacity = max(2, 4 * rows // (local * groups))
    cap = -(-capacity // 16) * 16
    nx = math.isqrt(fsdp)
    ny = fsdp // nx
    slots = groups * local * cap
    w_in = jnp.transpose(weight_in, (1, 0, 2))
    w_out = jnp.transpose(weight_out, (1, 0, 2))
    shard_in, shard_out = (drows, hidden), (hrows, feature)
    exchange = (groups, local, 2, cap, feature)
    swapped = (local, groups, 2, cap, feature)
    vmem = pl.BlockSpec(memory_space=pltpu.VMEM)
    dma = pltpu.SemaphoreType.DMA
    defect, grad_states, grad_in, grad_out = pl.pallas_call(
        functools.partial(kernel, (groups, fsdp, nx, ny, local, cap)),
        out_shape=(
            jax.ShapeDtypeStruct((rows, feature), BF),
            jax.ShapeDtypeStruct((rows, feature), BF),
            jax.ShapeDtypeStruct((local,) + shard_in, BF),
            jax.ShapeDtypeStruct((local,) + shard_out, BF),
        ),
        in_specs=[vmem] * 7,
        out_specs=(vmem,) * 4,
        scratch_shapes=[
            pltpu.VMEM(exchange, BF),
            pltpu.VMEM(swapped, BF),
            pltpu.VMEM(swapped, BF),
            pltpu.VMEM(exchange, BF),
            pltpu.VMEM((fsdp,) + shard_in, BF),
            pltpu.VMEM((fsdp,) + shard_out, BF),
            pltpu.VMEM((fsdp,) + shard_in, BF),
            pltpu.VMEM((fsdp,) + shard_out, BF),
            pltpu.VMEM((ny, nx) + shard_in, BF),
            pltpu.VMEM((ny, nx) + shard_out, BF),
            pltpu.VMEM((nx,) + shard_in, BF),
            pltpu.VMEM((nx,) + shard_out, BF),
            pltpu.VMEM((nx,) + shard_in, BF),
            pltpu.VMEM((nx,) + shard_out, BF),
            pltpu.VMEM((local * groups * cap, feature), F32),
            pltpu.VMEM((local * groups * cap, feature), F32),
            pltpu.VMEM((2, slots, rows), BF),
            dma((groups, local)),
            dma((local, groups)),
            dma((local, groups)),
            dma((groups, local)),
            dma((2, fsdp + nx)),
            dma((2, fsdp)),
            dma((2, ny, nx, ny)),
            dma((2, ny, nx, ny)),
            dma((2, nx)),
            dma((2, nx)),
        ],
        compiler_params=pltpu.CompilerParams(
            collective_id=0, has_side_effects=True, vmem_limit_bytes=56 * 1024 * 1024
        ),
    )(states, rates, expert_ids.T, gate_weights.T, cotangent, w_in, w_out)
    return (
        defect,
        grad_states,
        jnp.transpose(grad_in, (1, 0, 2)),
        jnp.transpose(grad_out, (1, 0, 2)),
    )


def solution(mesh):
    placed = (
        P(("expert", "fsdp"), None),
        P(("expert", "fsdp"), None),
        P(("expert", "fsdp"), None),
        P(("expert", "fsdp"), None),
        P(("expert", "fsdp"), None),
        P("fsdp", "expert", None),
        P("fsdp", "expert", None),
    )
    return jax.shard_map(
        on_device,
        mesh=mesh,
        in_specs=placed,
        out_specs=(
            P(("expert", "fsdp"), None),
            P(("expert", "fsdp"), None),
            P("fsdp", "expert", None),
            P("fsdp", "expert", None),
        ),
        check_vma=False,
    )
```

```python
import functools
import math

import jax
import jax.numpy as jnp
from jax import lax
from jax.experimental import pallas as pl
from jax.experimental.pallas import tpu as pltpu
from jax.sharding import PartitionSpec as P

MESH = pl.DeviceIdType.MESH
BF = jnp.bfloat16
F32 = jnp.float32


def dot(left, right, left_dim, right_dim):
    return lax.dot_general(
        left, right, (((left_dim,), (right_dim,)), ((), ())), preferred_element_type=F32
    )


def kernel(
    sizes,
    states, rates, ids, gates, cotangent, w_in, w_out,
    defect, grad_states, grad_in, grad_out,
    tok_send, tok_recv, ret_send, ret_recv,
    full_in, full_out, part_in, part_out,
    first_in, first_out, sum_in, sum_out, second_in, second_out,
    acc_v, acc_r, picks, knots_t,
    tok_ss, tok_rs, ret_ss, ret_rs,
    w_ss, w_rs, one_ss, one_rs, two_ss, two_rs,
):
    groups, fsdp, nx, ny, local, cap = sizes
    rows, feature = states.shape
    hidden_all = w_in.shape[2]
    hrows = w_out.shape[1]
    slots = groups * local * cap
    lines = local * groups * cap
    sets = nx // local
    g = lax.axis_index("expert")
    f = lax.axis_index("fsdp")
    y, x = f // nx, lax.rem(f, nx)
    q, mine = x // local, lax.rem(x, local)
    span = hidden_all // ny

    shards = (w_in, w_out)
    fulls = (full_in, full_out)
    parts = (part_in, part_out)
    firsts = (first_in, first_out)
    sums = (sum_in, sum_out)
    seconds = (second_in, second_out)
    outs = (grad_in, grad_out)

    def turn(own, step, size):
        return lax.rem(own + step, size)

    def push(src, dst, send, recv, **device):
        return pltpu.make_async_remote_copy(
            src_ref=src, dst_ref=dst, send_sem=send, recv_sem=recv,
            device_id=device, device_id_type=MESH,
        )

    def greet(**device):
        pl.semaphore_signal(barrier, inc=1, device_id=device, device_id_type=MESH)

    def over_groups(start, act):
        def body(o, carry):
            act(o)
            return carry

        lax.fori_loop(start, groups, body, 0)

    def over_peers(act, order=1):
        for d in range(local)[::order]:
            over_groups(1 if d == 0 else 0, functools.partial(act, d))

    barrier = pltpu.get_barrier_semaphore()
    over_peers(
        lambda d, o: greet(
            expert=turn(g, o, groups), fsdp=y * nx + q * local + turn(mine, d, local)
        )
    )
    for k in range(1, sets):
        for d in range(local):
            greet(fsdp=y * nx + turn(q, k, sets) * local + d)
    for j in range(1, ny):
        greet(fsdp=turn(y, j, ny) * nx + x)
    def along_x(arr, i):
        to = turn(x, i, nx)
        return push(
            shards[arr].at[lax.rem(to, local)], fulls[arr].at[f],
            w_ss.at[arr, i - 1], w_rs.at[arr, f], fsdp=y * nx + to,
        )

    def along_y(arr, i, j):
        source = y * nx + turn(x, i, nx)
        src = shards[arr].at[mine] if i == 0 else fulls[arr].at[source]
        return push(
            src, fulls[arr].at[source], w_ss.at[arr, nx - 1 + i * (ny - 1) + j - 1],
            w_rs.at[arr, source], fsdp=turn(y, j, ny) * nx + x,
        )

    def shard_arrival(arr, i, j):
        source = turn(y, j, ny) * nx + turn(x, i, nx)
        return push(
            fulls[arr].at[source], fulls[arr].at[source], w_ss.at[arr, 0], w_rs.at[arr, source],
            fsdp=turn(y, j, ny) * nx + (x if j else turn(x, i, nx)),
        )

    experts_all = groups * local
    id_f = ids[...].astype(F32)
    gate = gates[...].T
    expert_iota = lax.broadcasted_iota(jnp.int32, (experts_all, rows), 0).astype(F32)
    hit = [(id_f[k:k + 1] == expert_iota).astype(F32) for k in range(2)]
    above = (
        lax.broadcasted_iota(jnp.int32, (rows, rows), 0)
        < lax.broadcasted_iota(jnp.int32, (rows, rows), 1)
    ).astype(F32).astype(BF)
    before = dot((hit[0] + hit[1]).astype(BF), above, 1, 0)
    slot_iota = lax.broadcasted_iota(jnp.int32, (slots, rows), 0).astype(F32)
    cot = cotangent[...].astype(F32)
    grads_slot = None
    for k in range(2):
        slot = jnp.sum(hit[k] * before, axis=0, keepdims=True)
        pick = (id_f[k:k + 1] * cap + slot == slot_iota).astype(F32).astype(BF)
        picks[k] = pick
        descent = (-gate[:, k:k + 1] * cot).astype(BF)
        term = dot(pick, descent, 1, 0)
        grads_slot = term if grads_slot is None else grads_slot + term
    shape = (groups, local, cap, feature)
    tok_send[:, :, 1] = grads_slot.astype(BF).reshape(shape)
    knots_slot = dot(picks[0] + picks[1], states[...], 1, 0)
    tok_send[:, :, 0] = knots_slot.astype(BF).reshape(shape)

    def tok_copy(d, o):
        other, e = turn(g, o, groups), turn(mine, d, local)
        return push(
            tok_send.at[other, e], tok_recv.at[mine, g], tok_ss.at[other, e], tok_rs.at[mine, g],
            expert=other, fsdp=y * nx + q * local + e,
        )

    def tok_arrival(d, o):
        other, e = turn(g, o, groups), turn(mine, d, local)
        return push(
            tok_send.at[other, e], tok_recv.at[e, other], tok_ss.at[other, e], tok_rs.at[e, other],
            expert=other, fsdp=y * nx + q * local + e,
        )

    pl.semaphore_wait(barrier, groups * local - 1 + nx - local + ny - 1)

    for arr in range(2):
        for i in range(1, nx):
            along_x(arr, i).start()
        for j in range(1, ny):
            along_y(arr, 0, j).start()
    over_peers(lambda d, o: tok_copy(d, o).start())
    tok_recv[mine, g] = tok_send[g, mine]
    for arr in range(2):
        fulls[arr][f] = shards[arr][mine]

    for arr in range(2):
        for i in range(1, nx):
            shard_arrival(arr, i, 0).wait_recv()
            for j in range(1, ny):
                along_y(arr, i, j).start()
    over_peers(lambda d, o: tok_arrival(d, o).wait_recv())
    for arr in range(2):
        for j in range(1, ny):
            for i in range(nx):
                shard_arrival(arr, i, j).wait_recv()

    width = max(256, hrows)
    per = width // hrows
    steps = span // width

    def one_copy(arr, j, i, row):
        there, column = turn(y, j, ny), turn(x, i, nx)
        shard = there * nx + column
        if arr == 1:
            return push(
                part_out.at[shard], first_out.at[y, column],
                one_ss.at[1, there, column, 0], one_rs.at[1, y, column, 0],
                fsdp=there * nx + x,
            )
        place = pl.ds(pl.multiple_of(row * span, span), span)
        return push(
            part_in.at[shard, :, place], first_in.at[y, column, :, place],
            one_ss.at[0, there, column, row], one_rs.at[0, y, column, row],
            fsdp=there * nx + x,
        )

    def one_arrival(arr, j, i, row):
        there, column = turn(y, j, ny), turn(x, i, nx)
        shard = there * nx + column
        if arr == 1:
            return push(
                part_out.at[shard], first_out.at[there, column],
                one_ss.at[1, there, column, 0], one_rs.at[1, there, column, 0],
                fsdp=there * nx + x,
            )
        place = pl.ds(pl.multiple_of(row * span, span), span)
        return push(
            part_in.at[shard, :, place], first_in.at[there, column, :, place],
            one_ss.at[0, there, column, row], one_rs.at[0, there, column, row],
            fsdp=there * nx + x,
        )

    knots_t[...] = tok_recv[:, :, 0].reshape(lines, feature).T
    acc_v[...] = jnp.zeros_like(acc_v)
    acc_r[...] = jnp.zeros_like(acc_r)
    for stage in range(1, ny + 1):
        row = turn(y, stage, ny)

        def chunk(c, carry):
            knots = tok_recv[:, :, 0].reshape(lines, feature)
            grads = tok_recv[:, :, 1].reshape(lines, feature)
            at = row * steps + c
            columns = pl.ds(pl.multiple_of(at * width, width), width)
            wi = full_in[:, :, columns].reshape(feature, width)
            wo = full_out[pl.ds(at * per, per)].reshape(width, feature)
            preact = dot(knots, wi, 1, 0)
            slope = dot(grads, wo, 1, 1)
            sigma = jax.nn.sigmoid(preact)
            hidden = (preact * sigma).astype(BF)
            inner = (slope * (sigma * (1.0 + preact * (1.0 - sigma)))).astype(BF)
            part_in[:, :, columns] = dot(knots_t[...], inner, 1, 0).astype(BF).reshape(
                fsdp, feature // fsdp, width
            )
            part_out[pl.ds(at * per, per)] = dot(hidden, grads, 0, 0).astype(BF).reshape(
                per, hrows, feature
            )
            acc_v[...] += dot(hidden, wo, 1, 0)
            acc_r[...] += dot(inner, wi, 1, 1)
            return carry

        lax.fori_loop(0, steps, chunk, 0)
        for i in range(1, nx):
            if stage < ny:
                one_copy(1, stage, i, 0).start()
            for j in range(1, ny):
                one_copy(0, j, i, row).start()

    for stage in range(1, ny + 1):
        for j in range(1, ny):
            one_copy(0, j, 0, turn(y, stage, ny)).start()
    for j in range(1, ny):
        one_copy(1, j, 0, 0).start()

    back = (local, groups, cap, feature)
    ret_send[:, :, 0] = acc_v[...].astype(BF).reshape(back)
    ret_send[:, :, 1] = acc_r[...].astype(BF).reshape(back)

    def ret_copy(d, o):
        other, c = turn(g, o, groups), turn(mine, d, local)
        return push(
            ret_send.at[c, other], ret_recv.at[g, mine], ret_ss.at[c, other], ret_rs.at[g, mine],
            expert=other, fsdp=y * nx + q * local + c,
        )

    def ret_arrival(d, o):
        other, c = turn(g, o, groups), turn(mine, d, local)
        return push(
            ret_send.at[c, other], ret_recv.at[other, c], ret_ss.at[c, other], ret_rs.at[other, c],
            expert=other, fsdp=y * nx + q * local + c,
        )

    over_peers(lambda d, o: ret_copy(d, o).start(), -1)
    ret_recv[g, mine] = ret_send[mine, g]

    def two_copy(arr, i):
        to = turn(x, i, nx)
        return push(
            sums[arr].at[to], seconds[arr].at[x], two_ss.at[arr, to], two_rs.at[arr, x],
            fsdp=y * nx + to,
        )

    def two_arrival(arr, source):
        return push(
            sums[arr].at[source], seconds[arr].at[source], two_ss.at[arr, source],
            two_rs.at[arr, source], fsdp=y * nx + source,
        )

    def summed(arr, i):
        column = turn(x, i, nx)
        total = parts[arr][y * nx + column].astype(F32)
        for j in range(1, ny):
            for row in range(ny if arr == 0 else 1):
                one_arrival(arr, j, i, row).wait_recv()
            total = total + firsts[arr][turn(y, j, ny), column].astype(F32)
        return total

    for i in range(1, nx):
        for arr in (1, 0):
            sums[arr][turn(x, i, nx)] = summed(arr, i).astype(BF)
            two_copy(arr, i).start()
    own = [summed(arr, 0) for arr in range(2)]
    for arr in range(2):
        total = own[arr]
        for k in range(1, sets):
            source = turn(q, k, sets) * local + mine
            two_arrival(arr, source).wait_recv()
            total = total + seconds[arr][source].astype(F32)
        outs[arr][mine] = total.astype(BF)

    over_peers(lambda d, o: ret_arrival(d, o).wait_recv())
    values = ret_recv[:, :, 0].reshape(slots, feature)
    combined = None
    for k in range(2):
        term = gate[:, k:k + 1] * dot(picks[k], values, 0, 0)
        combined = term if combined is None else combined + term
    defect[...] = (rates[...].astype(F32) - combined).astype(BF)
    returned = ret_recv[:, :, 1].reshape(slots, feature)
    grad_states[...] = dot(picks[0] + picks[1], returned, 0, 0).astype(BF)

    for d in range(1, local):
        e = turn(mine, d, local)
        for arr in (1, 0):
            total = None
            for k in range(sets):
                source = turn(q, k, sets) * local + e
                two_arrival(arr, source).wait_recv()
                term = seconds[arr][source].astype(F32)
                total = term if total is None else total + term
            outs[arr][e] = total.astype(BF)

    over_peers(lambda d, o: tok_copy(d, o).wait_send())
    over_peers(lambda d, o: ret_copy(d, o).wait_send())
    for arr in range(2):
        for i in range(1, nx):
            along_x(arr, i).wait_send()
            two_copy(arr, i).wait_send()
        for j in range(1, ny):
            for i in range(nx):
                along_y(arr, i, j).wait_send()
                for row in range(ny if arr == 0 else 1):
                    one_copy(arr, j, i, row).wait_send()


def on_device(states, rates, expert_ids, gate_weights, cotangent, weight_in, weight_out):
    groups, fsdp = lax.axis_size("expert"), lax.axis_size("fsdp")
    rows, feature = states.shape
    drows, local, hidden = weight_in.shape
    hrows = weight_out.shape[0]
    capacity = max(2, 4 * rows // (local * groups))
    cap = -(-capacity // 16) * 16
    nx = math.isqrt(fsdp)
    ny = fsdp // nx
    slots = groups * local * cap
    w_in = jnp.transpose(weight_in, (1, 0, 2))
    w_out = jnp.transpose(weight_out, (1, 0, 2))
    shard_in, shard_out = (drows, hidden), (hrows, feature)
    exchange = (groups, local, 2, cap, feature)
    swapped = (local, groups, 2, cap, feature)
    vmem = pl.BlockSpec(memory_space=pltpu.VMEM)
    dma = pltpu.SemaphoreType.DMA
    defect, grad_states, grad_in, grad_out = pl.pallas_call(
        functools.partial(kernel, (groups, fsdp, nx, ny, local, cap)),
        out_shape=(
            jax.ShapeDtypeStruct((rows, feature), BF),
            jax.ShapeDtypeStruct((rows, feature), BF),
            jax.ShapeDtypeStruct((local,) + shard_in, BF),
            jax.ShapeDtypeStruct((local,) + shard_out, BF),
        ),
        in_specs=[vmem] * 7,
        out_specs=(vmem,) * 4,
        scratch_shapes=[
            pltpu.VMEM(exchange, BF),
            pltpu.VMEM(swapped, BF),
            pltpu.VMEM(swapped, BF),
            pltpu.VMEM(exchange, BF),
            pltpu.VMEM((fsdp,) + shard_in, BF),
            pltpu.VMEM((fsdp,) + shard_out, BF),
            pltpu.VMEM((fsdp,) + shard_in, BF),
            pltpu.VMEM((fsdp,) + shard_out, BF),
            pltpu.VMEM((ny, nx) + shard_in, BF),
            pltpu.VMEM((ny, nx) + shard_out, BF),
            pltpu.VMEM((nx,) + shard_in, BF),
            pltpu.VMEM((nx,) + shard_out, BF),
            pltpu.VMEM((nx,) + shard_in, BF),
            pltpu.VMEM((nx,) + shard_out, BF),
            pltpu.VMEM((local * groups * cap, feature), F32),
            pltpu.VMEM((local * groups * cap, feature), F32),
            pltpu.VMEM((2, slots, rows), BF),
            pltpu.VMEM((feature, local * groups * cap), BF),
            dma((groups, local)),
            dma((local, groups)),
            dma((local, groups)),
            dma((groups, local)),
            dma((2, fsdp + nx)),
            dma((2, fsdp)),
            dma((2, ny, nx, ny)),
            dma((2, ny, nx, ny)),
            dma((2, nx)),
            dma((2, nx)),
        ],
        compiler_params=pltpu.CompilerParams(
            collective_id=0, has_side_effects=True, vmem_limit_bytes=36 * 1024 * 1024
        ),
    )(states, rates, expert_ids.T, gate_weights.T, cotangent, w_in, w_out)
    return (
        defect,
        grad_states,
        jnp.transpose(grad_in, (1, 0, 2)),
        jnp.transpose(grad_out, (1, 0, 2)),
    )


def solution(mesh):
    placed = (
        P(("expert", "fsdp"), None),
        P(("expert", "fsdp"), None),
        P(("expert", "fsdp"), None),
        P(("expert", "fsdp"), None),
        P(("expert", "fsdp"), None),
        P("fsdp", "expert", None),
        P("fsdp", "expert", None),
    )
    return jax.shard_map(
        on_device,
        mesh=mesh,
        in_specs=placed,
        out_specs=(
            P(("expert", "fsdp"), None),
            P(("expert", "fsdp"), None),
            P("fsdp", "expert", None),
            P("fsdp", "expert", None),
        ),
        check_vma=False,
    )
```

```python
import functools
import math

import jax
import jax.numpy as jnp
from jax import lax
from jax.experimental import pallas as pl
from jax.experimental.pallas import tpu as pltpu
from jax.sharding import PartitionSpec as P

MESH = pl.DeviceIdType.MESH
BF = jnp.bfloat16
F32 = jnp.float32


def dot(left, right, left_dim, right_dim):
    return lax.dot_general(
        left, right, (((left_dim,), (right_dim,)), ((), ())), preferred_element_type=F32
    )


def kernel(
    sizes,
    states, rates, ids, gates, cotangent, w_in, w_out,
    defect, grad_states, grad_in, grad_out,
    tok_send, tok_recv, ret_send, ret_recv,
    full_in, full_out, part_in, part_out,
    first_in, first_out, sum_in, sum_out, second_in, second_out,
    hid, inn, picks, knots_t,
    tok_ss, tok_rs, ret_ss, ret_rs,
    w_ss, w_rs, one_ss, one_rs, two_ss, two_rs,
):
    groups, fsdp, nx, ny, local, cap = sizes
    rows, feature = states.shape
    hidden_all = w_in.shape[2]
    hrows = w_out.shape[1]
    slots = groups * local * cap
    sets = nx // local
    g = lax.axis_index("expert")
    f = lax.axis_index("fsdp")
    y, x = f // nx, lax.rem(f, nx)
    q, mine = x // local, lax.rem(x, local)
    span = hidden_all // ny

    shards = (w_in, w_out)
    fulls = (full_in, full_out)
    parts = (part_in, part_out)
    firsts = (first_in, first_out)
    sums = (sum_in, sum_out)
    seconds = (second_in, second_out)
    outs = (grad_in, grad_out)

    def turn(own, step, size):
        return lax.rem(own + step, size)

    def push(src, dst, send, recv, **device):
        return pltpu.make_async_remote_copy(
            src_ref=src, dst_ref=dst, send_sem=send, recv_sem=recv,
            device_id=device, device_id_type=MESH,
        )

    def greet(**device):
        pl.semaphore_signal(barrier, inc=1, device_id=device, device_id_type=MESH)

    def over_groups(start, act):
        def body(o, carry):
            act(o)
            return carry

        lax.fori_loop(start, groups, body, 0)

    def over_peers(act, order=1):
        for d in range(local)[::order]:
            over_groups(1 if d == 0 else 0, functools.partial(act, d))

    barrier = pltpu.get_barrier_semaphore()
    over_peers(
        lambda d, o: greet(
            expert=turn(g, o, groups), fsdp=y * nx + q * local + turn(mine, d, local)
        )
    )
    for k in range(1, sets):
        for d in range(local):
            greet(fsdp=y * nx + turn(q, k, sets) * local + d)
    for j in range(1, ny):
        greet(fsdp=turn(y, j, ny) * nx + x)
    def along_x(arr, i):
        to = turn(x, i, nx)
        return push(
            shards[arr].at[lax.rem(to, local)], fulls[arr].at[f],
            w_ss.at[arr, i - 1], w_rs.at[arr, f], fsdp=y * nx + to,
        )

    def along_y(arr, i, j):
        source = y * nx + turn(x, i, nx)
        src = shards[arr].at[mine] if i == 0 else fulls[arr].at[source]
        return push(
            src, fulls[arr].at[source], w_ss.at[arr, nx - 1 + i * (ny - 1) + j - 1],
            w_rs.at[arr, source], fsdp=turn(y, j, ny) * nx + x,
        )

    def shard_arrival(arr, i, j):
        source = turn(y, j, ny) * nx + turn(x, i, nx)
        return push(
            fulls[arr].at[source], fulls[arr].at[source], w_ss.at[arr, 0], w_rs.at[arr, source],
            fsdp=turn(y, j, ny) * nx + (x if j else turn(x, i, nx)),
        )

    experts_all = groups * local
    id_f = ids[...].astype(F32)
    gate = gates[...].T
    expert_iota = lax.broadcasted_iota(jnp.int32, (experts_all, rows), 0).astype(F32)
    hit = [(id_f[k:k + 1] == expert_iota).astype(F32) for k in range(2)]
    above = (
        lax.broadcasted_iota(jnp.int32, (rows, rows), 0)
        < lax.broadcasted_iota(jnp.int32, (rows, rows), 1)
    ).astype(F32).astype(BF)
    before = dot((hit[0] + hit[1]).astype(BF), above, 1, 0)
    slot_iota = lax.broadcasted_iota(jnp.int32, (slots, rows), 0).astype(F32)
    cot = cotangent[...].astype(F32)
    grads_slot = None
    for k in range(2):
        slot = jnp.sum(hit[k] * before, axis=0, keepdims=True)
        pick = (id_f[k:k + 1] * cap + slot == slot_iota).astype(F32).astype(BF)
        picks[k] = pick
        descent = (-gate[:, k:k + 1] * cot).astype(BF)
        term = dot(pick, descent, 1, 0)
        grads_slot = term if grads_slot is None else grads_slot + term
    shape = (groups, local, cap, feature)
    tok_send[:, :, 1] = grads_slot.astype(BF).reshape(shape)
    knots_slot = dot(picks[0] + picks[1], states[...], 1, 0)
    tok_send[:, :, 0] = knots_slot.astype(BF).reshape(shape)

    def tok_copy(d, o):
        other, e = turn(g, o, groups), turn(mine, d, local)
        return push(
            tok_send.at[other, e], tok_recv.at[mine, g], tok_ss.at[other, e], tok_rs.at[mine, g],
            expert=other, fsdp=y * nx + q * local + e,
        )

    def tok_arrival(d, o):
        other, e = turn(g, o, groups), turn(mine, d, local)
        return push(
            tok_send.at[other, e], tok_recv.at[e, other], tok_ss.at[other, e], tok_rs.at[e, other],
            expert=other, fsdp=y * nx + q * local + e,
        )

    pl.semaphore_wait(barrier, groups * local - 1 + nx - local + ny - 1)

    for arr in range(2):
        for i in range(1, nx):
            along_x(arr, i).start()
        for j in range(1, ny):
            along_y(arr, 0, j).start()
    over_peers(lambda d, o: tok_copy(d, o).start())
    tok_recv[mine, g] = tok_send[g, mine]
    for arr in range(2):
        fulls[arr][f] = shards[arr][mine]

    for arr in range(2):
        for i in range(1, nx):
            shard_arrival(arr, i, 0).wait_recv()
            for j in range(1, ny):
                along_y(arr, i, j).start()
    for arr in range(2):
        for j in range(1, ny):
            for i in range(nx):
                shard_arrival(arr, i, j).wait_recv()

    def ret_copy(d, o):
        other, c = turn(g, o, groups), turn(mine, d, local)
        return push(
            ret_send.at[c, other], ret_recv.at[g, mine], ret_ss.at[c, other], ret_rs.at[g, mine],
            expert=other, fsdp=y * nx + q * local + c,
        )

    def ret_arrival(d, o):
        other, c = turn(g, o, groups), turn(mine, d, local)
        return push(
            ret_send.at[c, other], ret_recv.at[other, c], ret_ss.at[c, other], ret_rs.at[other, c],
            expert=other, fsdp=y * nx + q * local + c,
        )

    width = max(256, hrows)
    per = width // hrows
    steps = span // width
    lines = groups * cap
    for d in range(local):
        column = turn(mine, d, local)
        over_groups(0 if d else 1, lambda o: tok_arrival(d, o).wait_recv())

        def rows_chunk(c, carry):
            knots = tok_recv[column, :, 0].reshape(lines, feature)
            grads = tok_recv[column, :, 1].reshape(lines, feature)
            columns = pl.ds(pl.multiple_of(c * width, width), width)
            wi = full_in[:, :, columns].reshape(feature, width)
            wo = full_out[pl.ds(c * per, per)].reshape(width, feature)
            preact = dot(knots, wi, 1, 0)
            slope = dot(grads, wo, 1, 1)
            sigma = jax.nn.sigmoid(preact)
            hid[column, :, columns] = (preact * sigma).astype(BF)
            inn[column, :, columns] = (
                slope * (sigma * (1.0 + preact * (1.0 - sigma)))
            ).astype(BF)
            return carry

        lax.fori_loop(0, hidden_all // width, rows_chunk, 0)
        back = (groups, cap, feature)
        wo = full_out[...].reshape(hidden_all, feature)
        ret_send[column, :, 0] = dot(hid[column], wo, 1, 0).astype(BF).reshape(back)
        wi = full_in[...].reshape(feature, hidden_all)
        ret_send[column, :, 1] = dot(inn[column], wi, 1, 1).astype(BF).reshape(back)
        over_groups(0 if d else 1, lambda o: ret_copy(d, o).start())
        if d == 0:
            ret_recv[g, mine] = ret_send[mine, g]

    def one_copy(arr, j, i, row):
        there, column = turn(y, j, ny), turn(x, i, nx)
        shard = there * nx + column
        if arr == 1:
            return push(
                part_out.at[shard], first_out.at[y, column],
                one_ss.at[1, there, column, 0], one_rs.at[1, y, column, 0],
                fsdp=there * nx + x,
            )
        place = pl.ds(pl.multiple_of(row * span, span), span)
        return push(
            part_in.at[shard, :, place], first_in.at[y, column, :, place],
            one_ss.at[0, there, column, row], one_rs.at[0, y, column, row],
            fsdp=there * nx + x,
        )

    def one_arrival(arr, j, i, row):
        there, column = turn(y, j, ny), turn(x, i, nx)
        shard = there * nx + column
        if arr == 1:
            return push(
                part_out.at[shard], first_out.at[there, column],
                one_ss.at[1, there, column, 0], one_rs.at[1, there, column, 0],
                fsdp=there * nx + x,
            )
        place = pl.ds(pl.multiple_of(row * span, span), span)
        return push(
            part_in.at[shard, :, place], first_in.at[there, column, :, place],
            one_ss.at[0, there, column, row], one_rs.at[0, there, column, row],
            fsdp=there * nx + x,
        )

    knots_t[...] = tok_recv[:, :, 0].reshape(local * lines, feature).T
    for stage in range(1, ny + 1):
        row = turn(y, stage, ny)

        def grad_chunk(c, carry):
            grads = tok_recv[:, :, 1].reshape(local * lines, feature)
            at = row * steps + c
            columns = pl.ds(pl.multiple_of(at * width, width), width)
            hidden = hid[:, :, columns].reshape(local * lines, width)
            inner = inn[:, :, columns].reshape(local * lines, width)
            part_out[pl.ds(at * per, per)] = dot(hidden, grads, 0, 0).astype(BF).reshape(
                per, hrows, feature
            )
            part_in[:, :, columns] = dot(knots_t[...], inner, 1, 0).astype(BF).reshape(
                fsdp, feature // fsdp, width
            )
            return carry

        lax.fori_loop(0, steps, grad_chunk, 0)
        for i in range(1, nx):
            if stage < ny:
                one_copy(1, stage, i, 0).start()
            for j in range(1, ny):
                one_copy(0, j, i, row).start()

    for stage in range(1, ny + 1):
        for j in range(1, ny):
            one_copy(0, j, 0, turn(y, stage, ny)).start()
    for j in range(1, ny):
        one_copy(1, j, 0, 0).start()

    def two_copy(arr, i):
        to = turn(x, i, nx)
        return push(
            sums[arr].at[to], seconds[arr].at[x], two_ss.at[arr, to], two_rs.at[arr, x],
            fsdp=y * nx + to,
        )

    def two_arrival(arr, source):
        return push(
            sums[arr].at[source], seconds[arr].at[source], two_ss.at[arr, source],
            two_rs.at[arr, source], fsdp=y * nx + source,
        )

    def summed(arr, i):
        column = turn(x, i, nx)
        total = parts[arr][y * nx + column].astype(F32)
        for j in range(1, ny):
            for row in range(ny if arr == 0 else 1):
                one_arrival(arr, j, i, row).wait_recv()
            total = total + firsts[arr][turn(y, j, ny), column].astype(F32)
        return total

    for i in range(1, nx):
        for arr in (1, 0):
            sums[arr][turn(x, i, nx)] = summed(arr, i).astype(BF)
            two_copy(arr, i).start()
    own = [summed(arr, 0) for arr in range(2)]
    for arr in range(2):
        total = own[arr]
        for k in range(1, sets):
            source = turn(q, k, sets) * local + mine
            two_arrival(arr, source).wait_recv()
            total = total + seconds[arr][source].astype(F32)
        outs[arr][mine] = total.astype(BF)

    over_peers(lambda d, o: ret_arrival(d, o).wait_recv())
    values = ret_recv[:, :, 0].reshape(slots, feature)
    combined = None
    for k in range(2):
        term = gate[:, k:k + 1] * dot(picks[k], values, 0, 0)
        combined = term if combined is None else combined + term
    defect[...] = (rates[...].astype(F32) - combined).astype(BF)
    returned = ret_recv[:, :, 1].reshape(slots, feature)
    grad_states[...] = dot(picks[0] + picks[1], returned, 0, 0).astype(BF)

    for d in range(1, local):
        e = turn(mine, d, local)
        for arr in (1, 0):
            total = None
            for k in range(sets):
                source = turn(q, k, sets) * local + e
                two_arrival(arr, source).wait_recv()
                term = seconds[arr][source].astype(F32)
                total = term if total is None else total + term
            outs[arr][e] = total.astype(BF)

    over_peers(lambda d, o: tok_copy(d, o).wait_send())
    over_peers(lambda d, o: ret_copy(d, o).wait_send())
    for arr in range(2):
        for i in range(1, nx):
            along_x(arr, i).wait_send()
            two_copy(arr, i).wait_send()
        for j in range(1, ny):
            for i in range(nx):
                along_y(arr, i, j).wait_send()
                for row in range(ny if arr == 0 else 1):
                    one_copy(arr, j, i, row).wait_send()


def on_device(states, rates, expert_ids, gate_weights, cotangent, weight_in, weight_out):
    groups, fsdp = lax.axis_size("expert"), lax.axis_size("fsdp")
    rows, feature = states.shape
    drows, local, hidden = weight_in.shape
    hrows = weight_out.shape[0]
    capacity = max(2, 4 * rows // (local * groups))
    cap = -(-capacity // 16) * 16
    nx = math.isqrt(fsdp)
    ny = fsdp // nx
    slots = groups * local * cap
    w_in = jnp.transpose(weight_in, (1, 0, 2))
    w_out = jnp.transpose(weight_out, (1, 0, 2))
    shard_in, shard_out = (drows, hidden), (hrows, feature)
    exchange = (groups, local, 2, cap, feature)
    swapped = (local, groups, 2, cap, feature)
    vmem = pl.BlockSpec(memory_space=pltpu.VMEM)
    dma = pltpu.SemaphoreType.DMA
    defect, grad_states, grad_in, grad_out = pl.pallas_call(
        functools.partial(kernel, (groups, fsdp, nx, ny, local, cap)),
        out_shape=(
            jax.ShapeDtypeStruct((rows, feature), BF),
            jax.ShapeDtypeStruct((rows, feature), BF),
            jax.ShapeDtypeStruct((local,) + shard_in, BF),
            jax.ShapeDtypeStruct((local,) + shard_out, BF),
        ),
        in_specs=[vmem] * 7,
        out_specs=(vmem,) * 4,
        scratch_shapes=[
            pltpu.VMEM(exchange, BF),
            pltpu.VMEM(swapped, BF),
            pltpu.VMEM(swapped, BF),
            pltpu.VMEM(exchange, BF),
            pltpu.VMEM((fsdp,) + shard_in, BF),
            pltpu.VMEM((fsdp,) + shard_out, BF),
            pltpu.VMEM((fsdp,) + shard_in, BF),
            pltpu.VMEM((fsdp,) + shard_out, BF),
            pltpu.VMEM((ny, nx) + shard_in, BF),
            pltpu.VMEM((ny, nx) + shard_out, BF),
            pltpu.VMEM((nx,) + shard_in, BF),
            pltpu.VMEM((nx,) + shard_out, BF),
            pltpu.VMEM((nx,) + shard_in, BF),
            pltpu.VMEM((nx,) + shard_out, BF),
            pltpu.VMEM((local, groups * cap, hidden), BF),
            pltpu.VMEM((local, groups * cap, hidden), BF),
            pltpu.VMEM((2, slots, rows), BF),
            pltpu.VMEM((feature, local * groups * cap), BF),
            dma((groups, local)),
            dma((local, groups)),
            dma((local, groups)),
            dma((groups, local)),
            dma((2, fsdp + nx)),
            dma((2, fsdp)),
            dma((2, ny, nx, ny)),
            dma((2, ny, nx, ny)),
            dma((2, nx)),
            dma((2, nx)),
        ],
        compiler_params=pltpu.CompilerParams(
            collective_id=0, has_side_effects=True, vmem_limit_bytes=36 * 1024 * 1024
        ),
    )(states, rates, expert_ids.T, gate_weights.T, cotangent, w_in, w_out)
    return (
        defect,
        grad_states,
        jnp.transpose(grad_in, (1, 0, 2)),
        jnp.transpose(grad_out, (1, 0, 2)),
    )


def solution(mesh):
    placed = (
        P(("expert", "fsdp"), None),
        P(("expert", "fsdp"), None),
        P(("expert", "fsdp"), None),
        P(("expert", "fsdp"), None),
        P(("expert", "fsdp"), None),
        P("fsdp", "expert", None),
        P("fsdp", "expert", None),
    )
    return jax.shard_map(
        on_device,
        mesh=mesh,
        in_specs=placed,
        out_specs=(
            P(("expert", "fsdp"), None),
            P(("expert", "fsdp"), None),
            P("fsdp", "expert", None),
            P("fsdp", "expert", None),
        ),
        check_vma=False,
    )
```

```python
import functools
import math

import jax
import jax.numpy as jnp
from jax import lax
from jax.experimental import pallas as pl
from jax.experimental.pallas import tpu as pltpu
from jax.sharding import PartitionSpec as P

MESH = pl.DeviceIdType.MESH
BF = jnp.bfloat16
F32 = jnp.float32


def dot(left, right, left_dim, right_dim):
    return lax.dot_general(
        left, right, (((left_dim,), (right_dim,)), ((), ())), preferred_element_type=F32
    )


def kernel(
    sizes,
    states, rates, ids, gates, cotangent, w_in, w_out,
    defect, grad_states, grad_in, grad_out,
    tok_send, tok_recv, ret_send, ret_recv,
    full_in, full_out, part_in, part_out,
    first_in, first_out, sum_in, sum_out, second_in, second_out,
    acc_v, acc_r, picks, knots_t,
    tok_ss, tok_rs, ret_ss, ret_rs,
    w_ss, w_rs, one_ss, one_rs, two_ss, two_rs,
):
    groups, fsdp, nx, ny, local, cap = sizes
    rows, feature = states.shape
    hidden_all = w_in.shape[2]
    hrows = w_out.shape[1]
    slots = groups * local * cap
    lines = local * groups * cap
    sets = nx // local
    g = lax.axis_index("expert")
    f = lax.axis_index("fsdp")
    y, x = f // nx, lax.rem(f, nx)
    q, mine = x // local, lax.rem(x, local)
    span = hidden_all // ny

    shards = (w_in, w_out)
    fulls = (full_in, full_out)
    parts = (part_in, part_out)
    firsts = (first_in, first_out)
    sums = (sum_in, sum_out)
    seconds = (second_in, second_out)
    outs = (grad_in, grad_out)

    def turn(own, step, size):
        return lax.rem(own + step, size)

    def push(src, dst, send, recv, **device):
        return pltpu.make_async_remote_copy(
            src_ref=src, dst_ref=dst, send_sem=send, recv_sem=recv,
            device_id=device, device_id_type=MESH,
        )

    def greet(**device):
        pl.semaphore_signal(barrier, inc=1, device_id=device, device_id_type=MESH)

    def over_groups(start, act):
        def body(o, carry):
            act(o)
            return carry

        lax.fori_loop(start, groups, body, 0)

    def over_peers(act, order=1):
        for d in range(local)[::order]:
            over_groups(1 if d == 0 else 0, functools.partial(act, d))

    barrier = pltpu.get_barrier_semaphore()
    over_peers(
        lambda d, o: greet(
            expert=turn(g, o, groups), fsdp=y * nx + q * local + turn(mine, d, local)
        )
    )
    for k in range(1, sets):
        for d in range(local):
            greet(fsdp=y * nx + turn(q, k, sets) * local + d)
    for j in range(1, ny):
        greet(fsdp=turn(y, j, ny) * nx + x)
    def span_at(k):
        return pl.ds(pl.multiple_of(turn(y, k, ny) * span, span), span)

    def along_x(arr, i, k):
        to = turn(x, i, nx)
        src, dst = shards[arr].at[lax.rem(to, local)], fulls[arr].at[f]
        if arr == 0:
            src, dst = src.at[:, span_at(k)], dst.at[:, span_at(k)]
        return push(
            src, dst, w_ss.at[arr, i, 0, k], w_rs.at[arr, f, turn(y, k, ny) if arr == 0 else 0],
            fsdp=y * nx + to,
        )

    def along_y(arr, i, j, k):
        source = y * nx + turn(x, i, nx)
        src = shards[arr].at[mine] if i == 0 else fulls[arr].at[source]
        dst = fulls[arr].at[source]
        if arr == 0:
            src, dst = src.at[:, span_at(k)], dst.at[:, span_at(k)]
        return push(
            src, dst, w_ss.at[arr, i, j, k],
            w_rs.at[arr, source, turn(y, k, ny) if arr == 0 else 0],
            fsdp=turn(y, j, ny) * nx + x,
        )

    arrived = set()

    def await_shard(arr, i, j, k):
        if (i, j) == (0, 0) or (arr, i, j, k) in arrived:
            return
        arrived.add((arr, i, j, k))
        source = turn(y, j, ny) * nx + turn(x, i, nx)
        piece = fulls[arr].at[source]
        if arr == 0:
            piece = piece.at[:, span_at(k)]
        push(
            piece, piece, w_ss.at[arr, 0, 0, 0],
            w_rs.at[arr, source, turn(y, k, ny) if arr == 0 else 0],
            fsdp=turn(y, j, ny) * nx + (x if j else turn(x, i, nx)),
        ).wait_recv()

    def send_along_y(i, stage):
        for j in range(1, ny):
            if stage == ny - j:
                await_shard(1, i, 0, 0)
                along_y(1, i, j, 0).start()
            k = (j + stage) % ny
            await_shard(0, i, 0, k)
            along_y(0, i, j, k).start()

    experts_all = groups * local
    id_f = ids[...].astype(F32)
    gate = gates[...].T
    expert_iota = lax.broadcasted_iota(jnp.int32, (experts_all, rows), 0).astype(F32)
    hit = [(id_f[k:k + 1] == expert_iota).astype(F32) for k in range(2)]
    above = (
        lax.broadcasted_iota(jnp.int32, (rows, rows), 0)
        < lax.broadcasted_iota(jnp.int32, (rows, rows), 1)
    ).astype(F32).astype(BF)
    before = dot((hit[0] + hit[1]).astype(BF), above, 1, 0)
    slot_iota = lax.broadcasted_iota(jnp.int32, (slots, rows), 0).astype(F32)
    cot = cotangent[...].astype(F32)
    grads_slot = None
    for k in range(2):
        slot = jnp.sum(hit[k] * before, axis=0, keepdims=True)
        pick = (id_f[k:k + 1] * cap + slot == slot_iota).astype(F32).astype(BF)
        picks[k] = pick
        descent = (-gate[:, k:k + 1] * cot).astype(BF)
        term = dot(pick, descent, 1, 0)
        grads_slot = term if grads_slot is None else grads_slot + term
    shape = (groups, local, cap, feature)
    tok_send[:, :, 1] = grads_slot.astype(BF).reshape(shape)
    knots_slot = dot(picks[0] + picks[1], states[...], 1, 0)
    tok_send[:, :, 0] = knots_slot.astype(BF).reshape(shape)

    def tok_copy(d, o):
        other, e = turn(g, o, groups), turn(mine, d, local)
        return push(
            tok_send.at[other, e], tok_recv.at[mine, g], tok_ss.at[other, e], tok_rs.at[mine, g],
            expert=other, fsdp=y * nx + q * local + e,
        )

    def tok_arrival(d, o):
        other, e = turn(g, o, groups), turn(mine, d, local)
        return push(
            tok_send.at[other, e], tok_recv.at[e, other], tok_ss.at[other, e], tok_rs.at[e, other],
            expert=other, fsdp=y * nx + q * local + e,
        )

    pl.semaphore_wait(barrier, groups * local - 1 + nx - local + ny - 1)

    for i in range(1, nx):
        along_x(1, i, 0).start()
    send_along_y(0, 1)
    for k in range(ny):
        for i in range(1, nx):
            along_x(0, i, k).start()
    over_peers(lambda d, o: tok_copy(d, o).start())
    tok_recv[mine, g] = tok_send[g, mine]
    for arr in range(2):
        fulls[arr][f] = shards[arr][mine]

    for i in range(1, nx):
        send_along_y(i, 1)
    for stage in range(2, ny + 1):
        for i in range(nx):
            send_along_y(i, stage)
    over_peers(lambda d, o: tok_arrival(d, o).wait_recv())

    width = max(256, hrows)
    per = width // hrows
    steps = span // width

    def one_copy(arr, j, i, row):
        there, column = turn(y, j, ny), turn(x, i, nx)
        shard = there * nx + column
        if arr == 1:
            return push(
                part_out.at[shard], first_out.at[y, column],
                one_ss.at[1, there, column, 0], one_rs.at[1, y, column, 0],
                fsdp=there * nx + x,
            )
        place = pl.ds(pl.multiple_of(row * span, span), span)
        return push(
            part_in.at[shard, :, place], first_in.at[y, column, :, place],
            one_ss.at[0, there, column, row], one_rs.at[0, y, column, row],
            fsdp=there * nx + x,
        )

    def one_arrival(arr, j, i, row):
        there, column = turn(y, j, ny), turn(x, i, nx)
        shard = there * nx + column
        if arr == 1:
            return push(
                part_out.at[shard], first_out.at[there, column],
                one_ss.at[1, there, column, 0], one_rs.at[1, there, column, 0],
                fsdp=there * nx + x,
            )
        place = pl.ds(pl.multiple_of(row * span, span), span)
        return push(
            part_in.at[shard, :, place], first_in.at[there, column, :, place],
            one_ss.at[0, there, column, row], one_rs.at[0, there, column, row],
            fsdp=there * nx + x,
        )

    knots_t[...] = tok_recv[:, :, 0].reshape(lines, feature).T
    acc_v[...] = jnp.zeros_like(acc_v)
    acc_r[...] = jnp.zeros_like(acc_r)
    for stage in range(1, ny + 1):
        row = turn(y, stage, ny)
        for i in range(nx):
            await_shard(1, i, stage % ny, 0)
            for j in range(ny):
                await_shard(0, i, j, stage % ny)

        def chunk(c, carry):
            knots = tok_recv[:, :, 0].reshape(lines, feature)
            grads = tok_recv[:, :, 1].reshape(lines, feature)
            at = row * steps + c
            columns = pl.ds(pl.multiple_of(at * width, width), width)
            wi = full_in[:, :, columns].reshape(feature, width)
            wo = full_out[pl.ds(at * per, per)].reshape(width, feature)
            preact = dot(knots, wi, 1, 0)
            slope = dot(grads, wo, 1, 1)
            sigma = jax.nn.sigmoid(preact)
            hidden = (preact * sigma).astype(BF)
            inner = (slope * (sigma * (1.0 + preact * (1.0 - sigma)))).astype(BF)
            part_in[:, :, columns] = dot(knots_t[...], inner, 1, 0).astype(BF).reshape(
                fsdp, feature // fsdp, width
            )
            part_out[pl.ds(at * per, per)] = dot(hidden, grads, 0, 0).astype(BF).reshape(
                per, hrows, feature
            )
            acc_v[...] += dot(hidden, wo, 1, 0)
            acc_r[...] += dot(inner, wi, 1, 1)
            return carry

        lax.fori_loop(0, steps, chunk, 0)
        for i in range(1, nx):
            if stage < ny:
                one_copy(1, stage, i, 0).start()
            for j in range(1, ny):
                one_copy(0, j, i, row).start()

    for stage in range(1, ny + 1):
        for j in range(1, ny):
            one_copy(0, j, 0, turn(y, stage, ny)).start()
    for j in range(1, ny):
        one_copy(1, j, 0, 0).start()

    back = (local, groups, cap, feature)
    ret_send[:, :, 0] = acc_v[...].astype(BF).reshape(back)
    ret_send[:, :, 1] = acc_r[...].astype(BF).reshape(back)

    def ret_copy(d, o):
        other, c = turn(g, o, groups), turn(mine, d, local)
        return push(
            ret_send.at[c, other], ret_recv.at[g, mine], ret_ss.at[c, other], ret_rs.at[g, mine],
            expert=other, fsdp=y * nx + q * local + c,
        )

    def ret_arrival(d, o):
        other, c = turn(g, o, groups), turn(mine, d, local)
        return push(
            ret_send.at[c, other], ret_recv.at[other, c], ret_ss.at[c, other], ret_rs.at[other, c],
            expert=other, fsdp=y * nx + q * local + c,
        )

    over_peers(lambda d, o: ret_copy(d, o).start(), -1)
    ret_recv[g, mine] = ret_send[mine, g]

    def two_copy(arr, i, k):
        to = turn(x, i, nx)
        src, dst = sums[arr].at[to], seconds[arr].at[x]
        if arr == 0:
            src, dst = src.at[:, span_at(k)], dst.at[:, span_at(k)]
        return push(
            src, dst, two_ss.at[arr, to, k], two_rs.at[arr, x, k], fsdp=y * nx + to,
        )

    def two_arrival(arr, source):
        for k in range(ny if arr == 0 else 1):
            piece = seconds[arr].at[source]
            if arr == 0:
                piece = piece.at[:, span_at(k)]
            push(
                piece, piece, two_ss.at[arr, source, k], two_rs.at[arr, source, k],
                fsdp=y * nx + source,
            ).wait_recv()

    def summed(arr, i, k):
        column = turn(x, i, nx)
        place = span_at(k) if arr == 0 else slice(None)
        total = parts[arr][y * nx + column, :, place].astype(F32)
        for j in range(1, ny):
            one_arrival(arr, j, i, turn(y, k, ny)).wait_recv()
            total = total + firsts[arr][turn(y, j, ny), column, :, place].astype(F32)
        return total

    for arr, k in [(1, 0)] + [(0, k) for k in range(ny)]:
        place = span_at(k) if arr == 0 else slice(None)
        for i in range(1, nx):
            sums[arr][turn(x, i, nx), :, place] = summed(arr, i, k).astype(BF)
            two_copy(arr, i, k).start()
    for arr, k in [(0, k) for k in range(ny)] + [(1, 0)]:
        place = span_at(k) if arr == 0 else slice(None)
        total = summed(arr, 0, k)
        for other in range(1, sets):
            source = turn(q, other, sets) * local + mine
            if k == 0:
                two_arrival(arr, source)
            total = total + seconds[arr][source, :, place].astype(F32)
        outs[arr][mine, :, place] = total.astype(BF)

    over_peers(lambda d, o: ret_arrival(d, o).wait_recv())
    values = ret_recv[:, :, 0].reshape(slots, feature)
    combined = None
    for k in range(2):
        term = gate[:, k:k + 1] * dot(picks[k], values, 0, 0)
        combined = term if combined is None else combined + term
    defect[...] = (rates[...].astype(F32) - combined).astype(BF)
    returned = ret_recv[:, :, 1].reshape(slots, feature)
    grad_states[...] = dot(picks[0] + picks[1], returned, 0, 0).astype(BF)

    for d in range(1, local):
        e = turn(mine, d, local)
        for arr in (1, 0):
            total = None
            for k in range(sets):
                source = turn(q, k, sets) * local + e
                two_arrival(arr, source)
                term = seconds[arr][source].astype(F32)
                total = term if total is None else total + term
            outs[arr][e] = total.astype(BF)

    over_peers(lambda d, o: tok_copy(d, o).wait_send())
    over_peers(lambda d, o: ret_copy(d, o).wait_send())
    for arr in range(2):
        for i in range(1, nx):
            for k in range(ny if arr == 0 else 1):
                along_x(arr, i, k).wait_send()
                two_copy(arr, i, k).wait_send()
        for j in range(1, ny):
            for i in range(nx):
                for k in range(ny if arr == 0 else 1):
                    along_y(arr, i, j, k).wait_send()
                for row in range(ny if arr == 0 else 1):
                    one_copy(arr, j, i, row).wait_send()


def on_device(states, rates, expert_ids, gate_weights, cotangent, weight_in, weight_out):
    groups, fsdp = lax.axis_size("expert"), lax.axis_size("fsdp")
    rows, feature = states.shape
    drows, local, hidden = weight_in.shape
    hrows = weight_out.shape[0]
    capacity = max(2, 4 * rows // (local * groups))
    cap = -(-capacity // 16) * 16
    nx = math.isqrt(fsdp)
    ny = fsdp // nx
    slots = groups * local * cap
    w_in = jnp.transpose(weight_in, (1, 0, 2))
    w_out = jnp.transpose(weight_out, (1, 0, 2))
    shard_in, shard_out = (drows, hidden), (hrows, feature)
    exchange = (groups, local, 2, cap, feature)
    swapped = (local, groups, 2, cap, feature)
    vmem = pl.BlockSpec(memory_space=pltpu.VMEM)
    dma = pltpu.SemaphoreType.DMA
    defect, grad_states, grad_in, grad_out = pl.pallas_call(
        functools.partial(kernel, (groups, fsdp, nx, ny, local, cap)),
        out_shape=(
            jax.ShapeDtypeStruct((rows, feature), BF),
            jax.ShapeDtypeStruct((rows, feature), BF),
            jax.ShapeDtypeStruct((local,) + shard_in, BF),
            jax.ShapeDtypeStruct((local,) + shard_out, BF),
        ),
        in_specs=[vmem] * 7,
        out_specs=(vmem,) * 4,
        scratch_shapes=[
            pltpu.VMEM(exchange, BF),
            pltpu.VMEM(swapped, BF),
            pltpu.VMEM(swapped, BF),
            pltpu.VMEM(exchange, BF),
            pltpu.VMEM((fsdp,) + shard_in, BF),
            pltpu.VMEM((fsdp,) + shard_out, BF),
            pltpu.VMEM((fsdp,) + shard_in, BF),
            pltpu.VMEM((fsdp,) + shard_out, BF),
            pltpu.VMEM((ny, nx) + shard_in, BF),
            pltpu.VMEM((ny, nx) + shard_out, BF),
            pltpu.VMEM((nx,) + shard_in, BF),
            pltpu.VMEM((nx,) + shard_out, BF),
            pltpu.VMEM((nx,) + shard_in, BF),
            pltpu.VMEM((nx,) + shard_out, BF),
            pltpu.VMEM((local * groups * cap, feature), F32),
            pltpu.VMEM((local * groups * cap, feature), F32),
            pltpu.VMEM((2, slots, rows), BF),
            pltpu.VMEM((feature, local * groups * cap), BF),
            dma((groups, local)),
            dma((local, groups)),
            dma((local, groups)),
            dma((groups, local)),
            dma((2, nx, ny, ny)),
            dma((2, fsdp, ny)),
            dma((2, ny, nx, ny)),
            dma((2, ny, nx, ny)),
            dma((2, nx, ny)),
            dma((2, nx, ny)),
        ],
        compiler_params=pltpu.CompilerParams(
            collective_id=0, has_side_effects=True, vmem_limit_bytes=36 * 1024 * 1024
        ),
    )(states, rates, expert_ids.T, gate_weights.T, cotangent, w_in, w_out)
    return (
        defect,
        grad_states,
        jnp.transpose(grad_in, (1, 0, 2)),
        jnp.transpose(grad_out, (1, 0, 2)),
    )


def solution(mesh):
    placed = (
        P(("expert", "fsdp"), None),
        P(("expert", "fsdp"), None),
        P(("expert", "fsdp"), None),
        P(("expert", "fsdp"), None),
        P(("expert", "fsdp"), None),
        P("fsdp", "expert", None),
        P("fsdp", "expert", None),
    )
    return jax.shard_map(
        on_device,
        mesh=mesh,
        in_specs=placed,
        out_specs=(
            P(("expert", "fsdp"), None),
            P(("expert", "fsdp"), None),
            P("fsdp", "expert", None),
            P("fsdp", "expert", None),
        ),
        check_vma=False,
    )
```

```python
import functools
import math

import jax
import jax.numpy as jnp
from jax import lax
from jax.experimental import pallas as pl
from jax.experimental.pallas import tpu as pltpu
from jax.sharding import PartitionSpec as P

MESH = pl.DeviceIdType.MESH
BF = jnp.bfloat16
F32 = jnp.float32


def dot(left, right, left_dim, right_dim):
    return lax.dot_general(
        left, right, (((left_dim,), (right_dim,)), ((), ())), preferred_element_type=F32
    )


def kernel(
    sizes,
    states, rates, ids, gates, cotangent, w_in, w_out,
    defect, grad_states, grad_in, grad_out,
    tok_send, tok_recv, ret_send, ret_recv,
    full_in, full_out, part_in, part_out,
    first_in, first_out, sum_in, sum_out, second_in, second_out,
    hid, inn, acc_v, acc_r, picks, knots_t,
    tok_ss, tok_rs, ret_ss, ret_rs,
    w_ss, w_rs, one_ss, one_rs, two_ss, two_rs,
):
    groups, fsdp, nx, ny, local, cap = sizes
    rows, feature = states.shape
    hidden_all = w_in.shape[2]
    hrows = w_out.shape[1]
    slots = groups * local * cap
    sets = nx // local
    g = lax.axis_index("expert")
    f = lax.axis_index("fsdp")
    y, x = f // nx, lax.rem(f, nx)
    q, mine = x // local, lax.rem(x, local)
    span = hidden_all // ny

    shards = (w_in, w_out)
    fulls = (full_in, full_out)
    parts = (part_in, part_out)
    firsts = (first_in, first_out)
    sums = (sum_in, sum_out)
    seconds = (second_in, second_out)
    outs = (grad_in, grad_out)

    def turn(own, step, size):
        return lax.rem(own + step, size)

    def push(src, dst, send, recv, **device):
        return pltpu.make_async_remote_copy(
            src_ref=src, dst_ref=dst, send_sem=send, recv_sem=recv,
            device_id=device, device_id_type=MESH,
        )

    def greet(**device):
        pl.semaphore_signal(barrier, inc=1, device_id=device, device_id_type=MESH)

    def over_groups(start, act):
        def body(o, carry):
            act(o)
            return carry

        lax.fori_loop(start, groups, body, 0)

    def over_peers(act, order=1):
        for d in range(local)[::order]:
            over_groups(1 if d == 0 else 0, functools.partial(act, d))

    barrier = pltpu.get_barrier_semaphore()
    over_peers(
        lambda d, o: greet(
            expert=turn(g, o, groups), fsdp=y * nx + q * local + turn(mine, d, local)
        )
    )
    for k in range(1, sets):
        for d in range(local):
            greet(fsdp=y * nx + turn(q, k, sets) * local + d)
    for j in range(1, ny):
        greet(fsdp=turn(y, j, ny) * nx + x)
    def span_at(k):
        return pl.ds(pl.multiple_of(turn(y, k, ny) * span, span), span)

    def along_x(arr, i, k):
        to = turn(x, i, nx)
        src, dst = shards[arr].at[lax.rem(to, local)], fulls[arr].at[f]
        if arr == 0:
            src, dst = src.at[:, span_at(k)], dst.at[:, span_at(k)]
        return push(
            src, dst, w_ss.at[arr, i, 0, k], w_rs.at[arr, f, turn(y, k, ny) if arr == 0 else 0],
            fsdp=y * nx + to,
        )

    def along_y(arr, i, j, k):
        source = y * nx + turn(x, i, nx)
        src = shards[arr].at[mine] if i == 0 else fulls[arr].at[source]
        dst = fulls[arr].at[source]
        if arr == 0:
            src, dst = src.at[:, span_at(k)], dst.at[:, span_at(k)]
        return push(
            src, dst, w_ss.at[arr, i, j, k],
            w_rs.at[arr, source, turn(y, k, ny) if arr == 0 else 0],
            fsdp=turn(y, j, ny) * nx + x,
        )

    arrived = set()

    def await_shard(arr, i, j, k):
        if (i, j) == (0, 0) or (arr, i, j, k) in arrived:
            return
        arrived.add((arr, i, j, k))
        source = turn(y, j, ny) * nx + turn(x, i, nx)
        piece = fulls[arr].at[source]
        if arr == 0:
            piece = piece.at[:, span_at(k)]
        push(
            piece, piece, w_ss.at[arr, 0, 0, 0],
            w_rs.at[arr, source, turn(y, k, ny) if arr == 0 else 0],
            fsdp=turn(y, j, ny) * nx + (x if j else turn(x, i, nx)),
        ).wait_recv()

    def send_along_y(i, stage):
        for j in range(1, ny):
            if stage == ny - j:
                await_shard(1, i, 0, 0)
                along_y(1, i, j, 0).start()
            k = (j + stage) % ny
            await_shard(0, i, 0, k)
            along_y(0, i, j, k).start()

    experts_all = groups * local
    id_f = ids[...].astype(F32)
    gate = gates[...].T
    expert_iota = lax.broadcasted_iota(jnp.int32, (experts_all, rows), 0).astype(F32)
    hit = [(id_f[k:k + 1] == expert_iota).astype(F32) for k in range(2)]
    above = (
        lax.broadcasted_iota(jnp.int32, (rows, rows), 0)
        < lax.broadcasted_iota(jnp.int32, (rows, rows), 1)
    ).astype(F32).astype(BF)
    before = dot((hit[0] + hit[1]).astype(BF), above, 1, 0)
    slot_iota = lax.broadcasted_iota(jnp.int32, (slots, rows), 0).astype(F32)
    cot = cotangent[...].astype(F32)
    grads_slot = None
    for k in range(2):
        slot = jnp.sum(hit[k] * before, axis=0, keepdims=True)
        pick = (id_f[k:k + 1] * cap + slot == slot_iota).astype(F32).astype(BF)
        picks[k] = pick
        descent = (-gate[:, k:k + 1] * cot).astype(BF)
        term = dot(pick, descent, 1, 0)
        grads_slot = term if grads_slot is None else grads_slot + term
    shape = (groups, local, cap, feature)
    tok_send[:, :, 1] = grads_slot.astype(BF).reshape(shape)
    knots_slot = dot(picks[0] + picks[1], states[...], 1, 0)
    tok_send[:, :, 0] = knots_slot.astype(BF).reshape(shape)

    def tok_copy(d, o):
        other, e = turn(g, o, groups), turn(mine, d, local)
        return push(
            tok_send.at[other, e], tok_recv.at[mine, g], tok_ss.at[other, e], tok_rs.at[mine, g],
            expert=other, fsdp=y * nx + q * local + e,
        )

    def tok_arrival(d, o):
        other, e = turn(g, o, groups), turn(mine, d, local)
        return push(
            tok_send.at[other, e], tok_recv.at[e, other], tok_ss.at[other, e], tok_rs.at[e, other],
            expert=other, fsdp=y * nx + q * local + e,
        )

    pl.semaphore_wait(barrier, groups * local - 1 + nx - local + ny - 1)

    for i in range(1, nx):
        along_x(1, i, 0).start()
    send_along_y(0, 1)
    for k in range(ny):
        for i in range(1, nx):
            along_x(0, i, k).start()
    over_peers(lambda d, o: tok_copy(d, o).start())
    tok_recv[mine, g] = tok_send[g, mine]
    for arr in range(2):
        fulls[arr][f] = shards[arr][mine]

    for i in range(1, nx):
        send_along_y(i, 1)
    for stage in range(2, ny + 1):
        for i in range(nx):
            send_along_y(i, stage)

    width = max(256, hrows)
    per = width // hrows
    steps = span // width
    lines = groups * cap

    def ret_copy(d, o):
        other, c = turn(g, o, groups), turn(mine, d, local)
        return push(
            ret_send.at[c, other], ret_recv.at[g, mine], ret_ss.at[c, other], ret_rs.at[g, mine],
            expert=other, fsdp=y * nx + q * local + c,
        )

    def ret_arrival(d, o):
        other, c = turn(g, o, groups), turn(mine, d, local)
        return push(
            ret_send.at[c, other], ret_recv.at[other, c], ret_ss.at[c, other], ret_rs.at[other, c],
            expert=other, fsdp=y * nx + q * local + c,
        )

    def one_copy(arr, j, i, row):
        there, column = turn(y, j, ny), turn(x, i, nx)
        shard = there * nx + column
        if arr == 1:
            return push(
                part_out.at[shard], first_out.at[y, column],
                one_ss.at[1, there, column, 0], one_rs.at[1, y, column, 0],
                fsdp=there * nx + x,
            )
        place = pl.ds(pl.multiple_of(row * span, span), span)
        return push(
            part_in.at[shard, :, place], first_in.at[y, column, :, place],
            one_ss.at[0, there, column, row], one_rs.at[0, y, column, row],
            fsdp=there * nx + x,
        )

    def one_arrival(arr, j, i, row):
        there, column = turn(y, j, ny), turn(x, i, nx)
        shard = there * nx + column
        if arr == 1:
            return push(
                part_out.at[shard], first_out.at[there, column],
                one_ss.at[1, there, column, 0], one_rs.at[1, there, column, 0],
                fsdp=there * nx + x,
            )
        place = pl.ds(pl.multiple_of(row * span, span), span)
        return push(
            part_in.at[shard, :, place], first_in.at[there, column, :, place],
            one_ss.at[0, there, column, row], one_rs.at[0, there, column, row],
            fsdp=there * nx + x,
        )

    acc_v[...] = jnp.zeros_like(acc_v)
    acc_r[...] = jnp.zeros_like(acc_r)

    def rows_of(column, row):
        def chunk(c, carry):
            knots = tok_recv[column, :, 0].reshape(lines, feature)
            grads = tok_recv[column, :, 1].reshape(lines, feature)
            at = row * steps + c
            columns = pl.ds(pl.multiple_of(at * width, width), width)
            wi = full_in[:, :, columns].reshape(feature, width)
            wo = full_out[pl.ds(at * per, per)].reshape(width, feature)
            preact = dot(knots, wi, 1, 0)
            slope = dot(grads, wo, 1, 1)
            sigma = jax.nn.sigmoid(preact)
            hidden = (preact * sigma).astype(BF)
            inner = (slope * (sigma * (1.0 + preact * (1.0 - sigma)))).astype(BF)
            hid[column, :, columns] = hidden
            inn[column, :, columns] = inner
            acc_v[column] += dot(hidden, wo, 1, 0)
            acc_r[column] += dot(inner, wi, 1, 1)
            return carry

        lax.fori_loop(0, steps, chunk, 0)

    def grads_of(row):
        def chunk(c, carry):
            grads = tok_recv[:, :, 1].reshape(local * lines, feature)
            at = row * steps + c
            columns = pl.ds(pl.multiple_of(at * width, width), width)
            hidden = hid[:, :, columns].reshape(local * lines, width)
            inner = inn[:, :, columns].reshape(local * lines, width)
            part_out[pl.ds(at * per, per)] = dot(hidden, grads, 0, 0).astype(BF).reshape(
                per, hrows, feature
            )
            part_in[:, :, columns] = dot(knots_t[...], inner, 1, 0).astype(BF).reshape(
                fsdp, feature // fsdp, width
            )
            return carry

        lax.fori_loop(0, steps, chunk, 0)

    for d in range(local):
        column = turn(mine, d, local)
        over_groups(0 if d else 1, lambda o: tok_arrival(d, o).wait_recv())
        knots_t[:, pl.ds(pl.multiple_of(column * lines, lines), lines)] = (
            tok_recv[column, :, 0].reshape(lines, feature).T
        )
        for stage in range(1, ny + 1):
            row = turn(y, stage, ny)
            for i in range(nx):
                await_shard(1, i, stage % ny, 0)
                for j in range(ny):
                    await_shard(0, i, j, stage % ny)
            rows_of(column, row)
            if stage == ny:
                back = (groups, cap, feature)
                ret_send[column, :, 0] = acc_v[column].astype(BF).reshape(back)
                ret_send[column, :, 1] = acc_r[column].astype(BF).reshape(back)
                over_groups(0 if d else 1, lambda o: ret_copy(d, o).start())
                if d == 0:
                    ret_recv[g, mine] = ret_send[mine, g]
            if d == local - 1:
                grads_of(row)
                for i in range(1, nx):
                    if stage < ny:
                        one_copy(1, stage, i, 0).start()
                    for j in range(1, ny):
                        one_copy(0, j, i, row).start()

    for stage in range(1, ny + 1):
        for j in range(1, ny):
            one_copy(0, j, 0, turn(y, stage, ny)).start()
    for j in range(1, ny):
        one_copy(1, j, 0, 0).start()

    def two_copy(arr, i, k):
        to = turn(x, i, nx)
        src, dst = sums[arr].at[to], seconds[arr].at[x]
        if arr == 0:
            src, dst = src.at[:, span_at(k)], dst.at[:, span_at(k)]
        return push(
            src, dst, two_ss.at[arr, to, k], two_rs.at[arr, x, k], fsdp=y * nx + to,
        )

    def two_arrival(arr, source):
        for k in range(ny if arr == 0 else 1):
            piece = seconds[arr].at[source]
            if arr == 0:
                piece = piece.at[:, span_at(k)]
            push(
                piece, piece, two_ss.at[arr, source, k], two_rs.at[arr, source, k],
                fsdp=y * nx + source,
            ).wait_recv()

    def summed(arr, i, k):
        column = turn(x, i, nx)
        place = span_at(k) if arr == 0 else slice(None)
        total = parts[arr][y * nx + column, :, place].astype(F32)
        for j in range(1, ny):
            one_arrival(arr, j, i, turn(y, k, ny)).wait_recv()
            total = total + firsts[arr][turn(y, j, ny), column, :, place].astype(F32)
        return total

    for arr, k in [(1, 0)] + [(0, k) for k in range(ny)]:
        place = span_at(k) if arr == 0 else slice(None)
        for i in range(1, nx):
            sums[arr][turn(x, i, nx), :, place] = summed(arr, i, k).astype(BF)
            two_copy(arr, i, k).start()
    for arr, k in [(0, k) for k in range(ny)] + [(1, 0)]:
        place = span_at(k) if arr == 0 else slice(None)
        total = summed(arr, 0, k)
        for other in range(1, sets):
            source = turn(q, other, sets) * local + mine
            if k == 0:
                two_arrival(arr, source)
            total = total + seconds[arr][source, :, place].astype(F32)
        outs[arr][mine, :, place] = total.astype(BF)

    over_peers(lambda d, o: ret_arrival(d, o).wait_recv())
    values = ret_recv[:, :, 0].reshape(slots, feature)
    combined = None
    for k in range(2):
        term = gate[:, k:k + 1] * dot(picks[k], values, 0, 0)
        combined = term if combined is None else combined + term
    defect[...] = (rates[...].astype(F32) - combined).astype(BF)
    returned = ret_recv[:, :, 1].reshape(slots, feature)
    grad_states[...] = dot(picks[0] + picks[1], returned, 0, 0).astype(BF)

    for d in range(1, local):
        e = turn(mine, d, local)
        for arr in (1, 0):
            total = None
            for k in range(sets):
                source = turn(q, k, sets) * local + e
                two_arrival(arr, source)
                term = seconds[arr][source].astype(F32)
                total = term if total is None else total + term
            outs[arr][e] = total.astype(BF)

    over_peers(lambda d, o: tok_copy(d, o).wait_send())
    over_peers(lambda d, o: ret_copy(d, o).wait_send())
    for arr in range(2):
        for i in range(1, nx):
            for k in range(ny if arr == 0 else 1):
                along_x(arr, i, k).wait_send()
                two_copy(arr, i, k).wait_send()
        for j in range(1, ny):
            for i in range(nx):
                for k in range(ny if arr == 0 else 1):
                    along_y(arr, i, j, k).wait_send()
                for row in range(ny if arr == 0 else 1):
                    one_copy(arr, j, i, row).wait_send()


def on_device(states, rates, expert_ids, gate_weights, cotangent, weight_in, weight_out):
    groups, fsdp = lax.axis_size("expert"), lax.axis_size("fsdp")
    rows, feature = states.shape
    drows, local, hidden = weight_in.shape
    hrows = weight_out.shape[0]
    capacity = max(2, 4 * rows // (local * groups))
    cap = -(-capacity // 16) * 16
    nx = math.isqrt(fsdp)
    ny = fsdp // nx
    slots = groups * local * cap
    w_in = jnp.transpose(weight_in, (1, 0, 2))
    w_out = jnp.transpose(weight_out, (1, 0, 2))
    shard_in, shard_out = (drows, hidden), (hrows, feature)
    exchange = (groups, local, 2, cap, feature)
    swapped = (local, groups, 2, cap, feature)
    vmem = pl.BlockSpec(memory_space=pltpu.VMEM)
    dma = pltpu.SemaphoreType.DMA
    defect, grad_states, grad_in, grad_out = pl.pallas_call(
        functools.partial(kernel, (groups, fsdp, nx, ny, local, cap)),
        out_shape=(
            jax.ShapeDtypeStruct((rows, feature), BF),
            jax.ShapeDtypeStruct((rows, feature), BF),
            jax.ShapeDtypeStruct((local,) + shard_in, BF),
            jax.ShapeDtypeStruct((local,) + shard_out, BF),
        ),
        in_specs=[vmem] * 7,
        out_specs=(vmem,) * 4,
        scratch_shapes=[
            pltpu.VMEM(exchange, BF),
            pltpu.VMEM(swapped, BF),
            pltpu.VMEM(swapped, BF),
            pltpu.VMEM(exchange, BF),
            pltpu.VMEM((fsdp,) + shard_in, BF),
            pltpu.VMEM((fsdp,) + shard_out, BF),
            pltpu.VMEM((fsdp,) + shard_in, BF),
            pltpu.VMEM((fsdp,) + shard_out, BF),
            pltpu.VMEM((ny, nx) + shard_in, BF),
            pltpu.VMEM((ny, nx) + shard_out, BF),
            pltpu.VMEM((nx,) + shard_in, BF),
            pltpu.VMEM((nx,) + shard_out, BF),
            pltpu.VMEM((nx,) + shard_in, BF),
            pltpu.VMEM((nx,) + shard_out, BF),
            pltpu.VMEM((local, groups * cap, hidden), BF),
            pltpu.VMEM((local, groups * cap, hidden), BF),
            pltpu.VMEM((local, groups * cap, feature), F32),
            pltpu.VMEM((local, groups * cap, feature), F32),
            pltpu.VMEM((2, slots, rows), BF),
            pltpu.VMEM((feature, local * groups * cap), BF),
            dma((groups, local)),
            dma((local, groups)),
            dma((local, groups)),
            dma((groups, local)),
            dma((2, nx, ny, ny)),
            dma((2, fsdp, ny)),
            dma((2, ny, nx, ny)),
            dma((2, ny, nx, ny)),
            dma((2, nx, ny)),
            dma((2, nx, ny)),
        ],
        compiler_params=pltpu.CompilerParams(
            collective_id=0, has_side_effects=True, vmem_limit_bytes=36 * 1024 * 1024
        ),
    )(states, rates, expert_ids.T, gate_weights.T, cotangent, w_in, w_out)
    return (
        defect,
        grad_states,
        jnp.transpose(grad_in, (1, 0, 2)),
        jnp.transpose(grad_out, (1, 0, 2)),
    )


def solution(mesh):
    placed = (
        P(("expert", "fsdp"), None),
        P(("expert", "fsdp"), None),
        P(("expert", "fsdp"), None),
        P(("expert", "fsdp"), None),
        P(("expert", "fsdp"), None),
        P("fsdp", "expert", None),
        P("fsdp", "expert", None),
    )
    return jax.shard_map(
        on_device,
        mesh=mesh,
        in_specs=placed,
        out_specs=(
            P(("expert", "fsdp"), None),
            P(("expert", "fsdp"), None),
            P("fsdp", "expert", None),
            P("fsdp", "expert", None),
        ),
        check_vma=False,
    )
```

```python
import functools
import math

import jax
import jax.numpy as jnp
from jax import lax
from jax.experimental import pallas as pl
from jax.experimental.pallas import tpu as pltpu
from jax.sharding import PartitionSpec as P

MESH = pl.DeviceIdType.MESH
BF = jnp.bfloat16
F32 = jnp.float32


def dot(left, right, left_dim, right_dim):
    return lax.dot_general(
        left, right, (((left_dim,), (right_dim,)), ((), ())), preferred_element_type=F32
    )


def kernel(
    sizes,
    states, rates, ids, gates, cotangent, w_in, w_out,
    defect, grad_states, grad_in, grad_out,
    tok_send, tok_recv, ret_send, ret_recv,
    full_in, full_out, part_in, part_out,
    first_in, first_out, sum_in, sum_out, second_in, second_out,
    hid, inn, acc_v, acc_r, picks, knots_t,
    tok_ss, tok_rs, ret_ss, ret_rs,
    w_ss, w_rs, one_ss, one_rs, two_ss, two_rs,
):
    groups, fsdp, nx, ny, local, cap = sizes
    rows, feature = states.shape
    hidden_all = w_in.shape[2]
    hrows = w_out.shape[1]
    slots = groups * local * cap
    sets = nx // local
    g = lax.axis_index("expert")
    f = lax.axis_index("fsdp")
    y, x = f // nx, lax.rem(f, nx)
    q, mine = x // local, lax.rem(x, local)
    span = hidden_all // ny

    shards = (w_in, w_out)
    fulls = (full_in, full_out)
    parts = (part_in, part_out)
    firsts = (first_in, first_out)
    sums = (sum_in, sum_out)
    seconds = (second_in, second_out)
    outs = (grad_in, grad_out)

    def turn(own, step, size):
        return lax.rem(own + step, size)

    def push(src, dst, send, recv, **device):
        return pltpu.make_async_remote_copy(
            src_ref=src, dst_ref=dst, send_sem=send, recv_sem=recv,
            device_id=device, device_id_type=MESH,
        )

    def greet(**device):
        pl.semaphore_signal(barrier, inc=1, device_id=device, device_id_type=MESH)

    def over_groups(start, act):
        def body(o, carry):
            act(o)
            return carry

        lax.fori_loop(start, groups, body, 0)

    def over_peers(act, order=1):
        for d in range(local)[::order]:
            over_groups(1 if d == 0 else 0, functools.partial(act, d))

    barrier = pltpu.get_barrier_semaphore()
    over_peers(
        lambda d, o: greet(
            expert=turn(g, o, groups), fsdp=y * nx + q * local + turn(mine, d, local)
        )
    )
    for k in range(1, sets):
        for d in range(local):
            greet(fsdp=y * nx + turn(q, k, sets) * local + d)
    for j in range(1, ny):
        greet(fsdp=turn(y, j, ny) * nx + x)
    def span_at(k):
        return pl.ds(pl.multiple_of(turn(y, k, ny) * span, span), span)

    def along_x(arr, i, k):
        to = turn(x, i, nx)
        src, dst = shards[arr].at[lax.rem(to, local)], fulls[arr].at[f]
        if arr == 0:
            src, dst = src.at[:, span_at(k)], dst.at[:, span_at(k)]
        return push(
            src, dst, w_ss.at[arr, i, 0, k], w_rs.at[arr, f, turn(y, k, ny) if arr == 0 else 0],
            fsdp=y * nx + to,
        )

    def along_y(arr, i, j, k):
        source = y * nx + turn(x, i, nx)
        src = shards[arr].at[mine] if i == 0 else fulls[arr].at[source]
        dst = fulls[arr].at[source]
        if arr == 0:
            src, dst = src.at[:, span_at(k)], dst.at[:, span_at(k)]
        return push(
            src, dst, w_ss.at[arr, i, j, k],
            w_rs.at[arr, source, turn(y, k, ny) if arr == 0 else 0],
            fsdp=turn(y, j, ny) * nx + x,
        )

    arrived = set()

    def await_shard(arr, i, j, k):
        if (i, j) == (0, 0) or (arr, i, j, k) in arrived:
            return
        arrived.add((arr, i, j, k))
        source = turn(y, j, ny) * nx + turn(x, i, nx)
        piece = fulls[arr].at[source]
        if arr == 0:
            piece = piece.at[:, span_at(k)]
        push(
            piece, piece, w_ss.at[arr, 0, 0, 0],
            w_rs.at[arr, source, turn(y, k, ny) if arr == 0 else 0],
            fsdp=turn(y, j, ny) * nx + (x if j else turn(x, i, nx)),
        ).wait_recv()

    def send_along_y(i, stage):
        for j in range(1, ny):
            if stage == ny - j:
                await_shard(1, i, 0, 0)
                along_y(1, i, j, 0).start()
            k = (j + stage) % ny
            await_shard(0, i, 0, k)
            along_y(0, i, j, k).start()

    experts_all = groups * local
    id_f = ids[...].astype(F32)
    gate = gates[...].T
    expert_iota = lax.broadcasted_iota(jnp.int32, (experts_all, rows), 0).astype(F32)
    hit = [(id_f[k:k + 1] == expert_iota).astype(F32) for k in range(2)]
    above = (
        lax.broadcasted_iota(jnp.int32, (rows, rows), 0)
        < lax.broadcasted_iota(jnp.int32, (rows, rows), 1)
    ).astype(F32).astype(BF)
    before = dot((hit[0] + hit[1]).astype(BF), above, 1, 0)
    slot_iota = lax.broadcasted_iota(jnp.int32, (slots, rows), 0).astype(F32)
    cot = cotangent[...].astype(F32)
    grads_slot = None
    for k in range(2):
        slot = jnp.sum(hit[k] * before, axis=0, keepdims=True)
        pick = (id_f[k:k + 1] * cap + slot == slot_iota).astype(F32).astype(BF)
        picks[k] = pick
        descent = (-gate[:, k:k + 1] * cot).astype(BF)
        term = dot(pick, descent, 1, 0)
        grads_slot = term if grads_slot is None else grads_slot + term
    shape = (groups, local, cap, feature)
    tok_send[:, :, 1] = grads_slot.astype(BF).reshape(shape)
    knots_slot = dot(picks[0] + picks[1], states[...], 1, 0)
    tok_send[:, :, 0] = knots_slot.astype(BF).reshape(shape)

    def tok_copy(d, o):
        other, e = turn(g, o, groups), turn(mine, d, local)
        return push(
            tok_send.at[other, e], tok_recv.at[mine, g], tok_ss.at[other, e], tok_rs.at[mine, g],
            expert=other, fsdp=y * nx + q * local + e,
        )

    def tok_arrival(d, o):
        other, e = turn(g, o, groups), turn(mine, d, local)
        return push(
            tok_send.at[other, e], tok_recv.at[e, other], tok_ss.at[other, e], tok_rs.at[e, other],
            expert=other, fsdp=y * nx + q * local + e,
        )

    pl.semaphore_wait(barrier, groups * local - 1 + nx - local + ny - 1)

    over_groups(1, lambda o: tok_copy(0, o).start())
    for i in range(1, nx):
        along_x(1, i, 0).start()
    send_along_y(0, 1)
    for k in range(ny):
        for i in range(1, nx):
            along_x(0, i, k).start()
    tok_recv[mine, g] = tok_send[g, mine]
    for arr in range(2):
        fulls[arr][f] = shards[arr][mine]

    for i in range(1, nx):
        send_along_y(i, 1)
    over_groups(1, lambda o: tok_copy(0, o).wait_send())
    for d in range(1, local):
        over_groups(0, lambda o: tok_copy(d, o).start())
    for stage in range(2, ny + 1):
        for i in range(nx):
            send_along_y(i, stage)

    width = max(256, hrows)
    per = width // hrows
    steps = span // width
    lines = groups * cap

    def ret_copy(d, o):
        other, c = turn(g, o, groups), turn(mine, d, local)
        return push(
            ret_send.at[c, other], ret_recv.at[g, mine], ret_ss.at[c, other], ret_rs.at[g, mine],
            expert=other, fsdp=y * nx + q * local + c,
        )

    def ret_arrival(d, o):
        other, c = turn(g, o, groups), turn(mine, d, local)
        return push(
            ret_send.at[c, other], ret_recv.at[other, c], ret_ss.at[c, other], ret_rs.at[other, c],
            expert=other, fsdp=y * nx + q * local + c,
        )

    def one_copy(arr, j, i, row):
        there, column = turn(y, j, ny), turn(x, i, nx)
        shard = there * nx + column
        if arr == 1:
            return push(
                part_out.at[shard], first_out.at[y, column],
                one_ss.at[1, there, column, 0], one_rs.at[1, y, column, 0],
                fsdp=there * nx + x,
            )
        place = pl.ds(pl.multiple_of(row * span, span), span)
        return push(
            part_in.at[shard, :, place], first_in.at[y, column, :, place],
            one_ss.at[0, there, column, row], one_rs.at[0, y, column, row],
            fsdp=there * nx + x,
        )

    def one_arrival(arr, j, i, row):
        there, column = turn(y, j, ny), turn(x, i, nx)
        shard = there * nx + column
        if arr == 1:
            return push(
                part_out.at[shard], first_out.at[there, column],
                one_ss.at[1, there, column, 0], one_rs.at[1, there, column, 0],
                fsdp=there * nx + x,
            )
        place = pl.ds(pl.multiple_of(row * span, span), span)
        return push(
            part_in.at[shard, :, place], first_in.at[there, column, :, place],
            one_ss.at[0, there, column, row], one_rs.at[0, there, column, row],
            fsdp=there * nx + x,
        )

    acc_v[...] = jnp.zeros_like(acc_v)
    acc_r[...] = jnp.zeros_like(acc_r)

    def rows_of(column, row):
        def chunk(c, carry):
            knots = tok_recv[column, :, 0].reshape(lines, feature)
            grads = tok_recv[column, :, 1].reshape(lines, feature)
            at = row * steps + c
            columns = pl.ds(pl.multiple_of(at * width, width), width)
            wi = full_in[:, :, columns].reshape(feature, width)
            wo = full_out[pl.ds(at * per, per)].reshape(width, feature)
            preact = dot(knots, wi, 1, 0)
            slope = dot(grads, wo, 1, 1)
            sigma = jax.nn.sigmoid(preact)
            hidden = (preact * sigma).astype(BF)
            inner = (slope * (sigma * (1.0 + preact * (1.0 - sigma)))).astype(BF)
            hid[column, :, columns] = hidden
            inn[column, :, columns] = inner
            acc_v[column] += dot(hidden, wo, 1, 0)
            acc_r[column] += dot(inner, wi, 1, 1)
            return carry

        lax.fori_loop(0, steps, chunk, 0)

    def grads_of(row):
        def chunk(c, carry):
            grads = tok_recv[:, :, 1].reshape(local * lines, feature)
            at = row * steps + c
            columns = pl.ds(pl.multiple_of(at * width, width), width)
            hidden = hid[:, :, columns].reshape(local * lines, width)
            inner = inn[:, :, columns].reshape(local * lines, width)
            part_out[pl.ds(at * per, per)] = dot(hidden, grads, 0, 0).astype(BF).reshape(
                per, hrows, feature
            )
            part_in[:, :, columns] = dot(knots_t[...], inner, 1, 0).astype(BF).reshape(
                fsdp, feature // fsdp, width
            )
            return carry

        lax.fori_loop(0, steps, chunk, 0)

    for d in range(local):
        column = turn(mine, d, local)
        over_groups(0 if d else 1, lambda o: tok_arrival(d, o).wait_recv())
        knots_t[:, pl.ds(pl.multiple_of(column * lines, lines), lines)] = (
            tok_recv[column, :, 0].reshape(lines, feature).T
        )
        for stage in range(1, ny + 1):
            row = turn(y, stage, ny)
            for i in range(nx):
                await_shard(1, i, stage % ny, 0)
                for j in range(ny):
                    await_shard(0, i, j, stage % ny)
            rows_of(column, row)
            if stage == ny:
                back = (groups, cap, feature)
                ret_send[column, :, 0] = acc_v[column].astype(BF).reshape(back)
                ret_send[column, :, 1] = acc_r[column].astype(BF).reshape(back)
                over_groups(0 if d else 1, lambda o: ret_copy(d, o).start())
                if d == 0:
                    ret_recv[g, mine] = ret_send[mine, g]
            if d == local - 1:
                grads_of(row)
                for i in range(1, nx):
                    if stage < ny:
                        one_copy(1, stage, i, 0).start()
                    for j in range(1, ny):
                        one_copy(0, j, i, row).start()

    for stage in range(1, ny + 1):
        for j in range(1, ny):
            one_copy(0, j, 0, turn(y, stage, ny)).start()
    for j in range(1, ny):
        one_copy(1, j, 0, 0).start()

    def two_copy(arr, i, k):
        to = turn(x, i, nx)
        src, dst = sums[arr].at[to], seconds[arr].at[x]
        if arr == 0:
            src, dst = src.at[:, span_at(k)], dst.at[:, span_at(k)]
        return push(
            src, dst, two_ss.at[arr, to, k], two_rs.at[arr, x, k], fsdp=y * nx + to,
        )

    def two_arrival(arr, source):
        for k in range(ny if arr == 0 else 1):
            piece = seconds[arr].at[source]
            if arr == 0:
                piece = piece.at[:, span_at(k)]
            push(
                piece, piece, two_ss.at[arr, source, k], two_rs.at[arr, source, k],
                fsdp=y * nx + source,
            ).wait_recv()

    def summed(arr, i, k):
        column = turn(x, i, nx)
        place = span_at(k) if arr == 0 else slice(None)
        total = parts[arr][y * nx + column, :, place].astype(F32)
        for j in range(1, ny):
            one_arrival(arr, j, i, turn(y, k, ny)).wait_recv()
            total = total + firsts[arr][turn(y, j, ny), column, :, place].astype(F32)
        return total

    for arr, k in [(1, 0)] + [(0, k) for k in range(ny)]:
        place = span_at(k) if arr == 0 else slice(None)
        for i in range(1, nx):
            sums[arr][turn(x, i, nx), :, place] = summed(arr, i, k).astype(BF)
            two_copy(arr, i, k).start()
    for arr, k in [(0, k) for k in range(ny)] + [(1, 0)]:
        place = span_at(k) if arr == 0 else slice(None)
        total = summed(arr, 0, k)
        for other in range(1, sets):
            source = turn(q, other, sets) * local + mine
            if k == 0:
                two_arrival(arr, source)
            total = total + seconds[arr][source, :, place].astype(F32)
        outs[arr][mine, :, place] = total.astype(BF)

    over_peers(lambda d, o: ret_arrival(d, o).wait_recv())
    values = ret_recv[:, :, 0].reshape(slots, feature)
    combined = None
    for k in range(2):
        term = gate[:, k:k + 1] * dot(picks[k], values, 0, 0)
        combined = term if combined is None else combined + term
    defect[...] = (rates[...].astype(F32) - combined).astype(BF)
    returned = ret_recv[:, :, 1].reshape(slots, feature)
    grad_states[...] = dot(picks[0] + picks[1], returned, 0, 0).astype(BF)

    for d in range(1, local):
        e = turn(mine, d, local)
        for arr in (1, 0):
            total = None
            for k in range(sets):
                source = turn(q, k, sets) * local + e
                two_arrival(arr, source)
                term = seconds[arr][source].astype(F32)
                total = term if total is None else total + term
            outs[arr][e] = total.astype(BF)

    for d in range(1, local):
        over_groups(0, lambda o: tok_copy(d, o).wait_send())
    over_peers(lambda d, o: ret_copy(d, o).wait_send())
    for arr in range(2):
        for i in range(1, nx):
            for k in range(ny if arr == 0 else 1):
                along_x(arr, i, k).wait_send()
                two_copy(arr, i, k).wait_send()
        for j in range(1, ny):
            for i in range(nx):
                for k in range(ny if arr == 0 else 1):
                    along_y(arr, i, j, k).wait_send()
                for row in range(ny if arr == 0 else 1):
                    one_copy(arr, j, i, row).wait_send()


def on_device(states, rates, expert_ids, gate_weights, cotangent, weight_in, weight_out):
    groups, fsdp = lax.axis_size("expert"), lax.axis_size("fsdp")
    rows, feature = states.shape
    drows, local, hidden = weight_in.shape
    hrows = weight_out.shape[0]
    capacity = max(2, 4 * rows // (local * groups))
    cap = -(-capacity // 16) * 16
    nx = math.isqrt(fsdp)
    ny = fsdp // nx
    slots = groups * local * cap
    w_in = jnp.transpose(weight_in, (1, 0, 2))
    w_out = jnp.transpose(weight_out, (1, 0, 2))
    shard_in, shard_out = (drows, hidden), (hrows, feature)
    exchange = (groups, local, 2, cap, feature)
    swapped = (local, groups, 2, cap, feature)
    vmem = pl.BlockSpec(memory_space=pltpu.VMEM)
    dma = pltpu.SemaphoreType.DMA
    defect, grad_states, grad_in, grad_out = pl.pallas_call(
        functools.partial(kernel, (groups, fsdp, nx, ny, local, cap)),
        out_shape=(
            jax.ShapeDtypeStruct((rows, feature), BF),
            jax.ShapeDtypeStruct((rows, feature), BF),
            jax.ShapeDtypeStruct((local,) + shard_in, BF),
            jax.ShapeDtypeStruct((local,) + shard_out, BF),
        ),
        in_specs=[vmem] * 7,
        out_specs=(vmem,) * 4,
        scratch_shapes=[
            pltpu.VMEM(exchange, BF),
            pltpu.VMEM(swapped, BF),
            pltpu.VMEM(swapped, BF),
            pltpu.VMEM(exchange, BF),
            pltpu.VMEM((fsdp,) + shard_in, BF),
            pltpu.VMEM((fsdp,) + shard_out, BF),
            pltpu.VMEM((fsdp,) + shard_in, BF),
            pltpu.VMEM((fsdp,) + shard_out, BF),
            pltpu.VMEM((ny, nx) + shard_in, BF),
            pltpu.VMEM((ny, nx) + shard_out, BF),
            pltpu.VMEM((nx,) + shard_in, BF),
            pltpu.VMEM((nx,) + shard_out, BF),
            pltpu.VMEM((nx,) + shard_in, BF),
            pltpu.VMEM((nx,) + shard_out, BF),
            pltpu.VMEM((local, groups * cap, hidden), BF),
            pltpu.VMEM((local, groups * cap, hidden), BF),
            pltpu.VMEM((local, groups * cap, feature), F32),
            pltpu.VMEM((local, groups * cap, feature), F32),
            pltpu.VMEM((2, slots, rows), BF),
            pltpu.VMEM((feature, local * groups * cap), BF),
            dma((groups, local)),
            dma((local, groups)),
            dma((local, groups)),
            dma((groups, local)),
            dma((2, nx, ny, ny)),
            dma((2, fsdp, ny)),
            dma((2, ny, nx, ny)),
            dma((2, ny, nx, ny)),
            dma((2, nx, ny)),
            dma((2, nx, ny)),
        ],
        compiler_params=pltpu.CompilerParams(
            collective_id=0, has_side_effects=True, vmem_limit_bytes=36 * 1024 * 1024
        ),
    )(states, rates, expert_ids.T, gate_weights.T, cotangent, w_in, w_out)
    return (
        defect,
        grad_states,
        jnp.transpose(grad_in, (1, 0, 2)),
        jnp.transpose(grad_out, (1, 0, 2)),
    )


def solution(mesh):
    placed = (
        P(("expert", "fsdp"), None),
        P(("expert", "fsdp"), None),
        P(("expert", "fsdp"), None),
        P(("expert", "fsdp"), None),
        P(("expert", "fsdp"), None),
        P("fsdp", "expert", None),
        P("fsdp", "expert", None),
    )
    return jax.shard_map(
        on_device,
        mesh=mesh,
        in_specs=placed,
        out_specs=(
            P(("expert", "fsdp"), None),
            P(("expert", "fsdp"), None),
            P("fsdp", "expert", None),
            P("fsdp", "expert", None),
        ),
        check_vma=False,
    )
```

```python
import functools
import math

import jax
import jax.numpy as jnp
from jax import lax
from jax.experimental import pallas as pl
from jax.experimental.pallas import tpu as pltpu
from jax.sharding import PartitionSpec as P

MESH = pl.DeviceIdType.MESH
BF = jnp.bfloat16
F32 = jnp.float32


def dot(left, right, left_dim, right_dim):
    return lax.dot_general(
        left, right, (((left_dim,), (right_dim,)), ((), ())), preferred_element_type=F32
    )


def kernel(
    sizes,
    states, rates, ids, gates, cotangent, w_in, w_out,
    defect, grad_states, grad_in, grad_out,
    tok_send, tok_recv, ret_send, ret_recv,
    full_in, full_out, part_in, part_out,
    first_in, first_out, sum_in, sum_out, second_in, second_out,
    acc_v, acc_r, picks, knots_t,
    tok_ss, tok_rs, ret_ss, ret_rs,
    w_ss, w_rs, one_ss, one_rs, two_ss, two_rs,
):
    groups, fsdp, nx, ny, local, cap = sizes
    rows, feature = states.shape
    hidden_all = w_in.shape[2]
    hrows = w_out.shape[1]
    slots = groups * local * cap
    lines = local * groups * cap
    sets = nx // local
    g = lax.axis_index("expert")
    f = lax.axis_index("fsdp")
    y, x = f // nx, lax.rem(f, nx)
    q, mine = x // local, lax.rem(x, local)
    span = hidden_all // ny

    shards = (w_in, w_out)
    fulls = (full_in, full_out)
    parts = (part_in, part_out)
    firsts = (first_in, first_out)
    sums = (sum_in, sum_out)
    seconds = (second_in, second_out)
    outs = (grad_in, grad_out)

    def turn(own, step, size):
        return lax.rem(own + step, size)

    def push(src, dst, send, recv, **device):
        return pltpu.make_async_remote_copy(
            src_ref=src, dst_ref=dst, send_sem=send, recv_sem=recv,
            device_id=device, device_id_type=MESH,
        )

    def greet(**device):
        pl.semaphore_signal(barrier, inc=1, device_id=device, device_id_type=MESH)

    def over_groups(start, act):
        def body(o, carry):
            act(o)
            return carry

        lax.fori_loop(start, groups, body, 0)

    def over_peers(act, order=1):
        for d in range(local)[::order]:
            over_groups(1 if d == 0 else 0, functools.partial(act, d))

    barrier = pltpu.get_barrier_semaphore()
    over_peers(
        lambda d, o: greet(
            expert=turn(g, o, groups), fsdp=y * nx + q * local + turn(mine, d, local)
        )
    )
    for k in range(1, sets):
        for d in range(local):
            greet(fsdp=y * nx + turn(q, k, sets) * local + d)
    for j in range(1, ny):
        greet(fsdp=turn(y, j, ny) * nx + x)
    def span_at(k):
        return pl.ds(pl.multiple_of(turn(y, k, ny) * span, span), span)

    def along_x(arr, i, k):
        to = turn(x, i, nx)
        src, dst = shards[arr].at[lax.rem(to, local)], fulls[arr].at[f]
        if arr == 0:
            src, dst = src.at[:, span_at(k)], dst.at[:, span_at(k)]
        return push(
            src, dst, w_ss.at[arr, i, 0, k], w_rs.at[arr, f, turn(y, k, ny) if arr == 0 else 0],
            fsdp=y * nx + to,
        )

    def along_y(arr, i, j, k):
        source = y * nx + turn(x, i, nx)
        src = shards[arr].at[mine] if i == 0 else fulls[arr].at[source]
        dst = fulls[arr].at[source]
        if arr == 0:
            src, dst = src.at[:, span_at(k)], dst.at[:, span_at(k)]
        return push(
            src, dst, w_ss.at[arr, i, j, k],
            w_rs.at[arr, source, turn(y, k, ny) if arr == 0 else 0],
            fsdp=turn(y, j, ny) * nx + x,
        )

    arrived = set()

    def await_shard(arr, i, j, k):
        if (i, j) == (0, 0) or (arr, i, j, k) in arrived:
            return
        arrived.add((arr, i, j, k))
        source = turn(y, j, ny) * nx + turn(x, i, nx)
        piece = fulls[arr].at[source]
        if arr == 0:
            piece = piece.at[:, span_at(k)]
        push(
            piece, piece, w_ss.at[arr, 0, 0, 0],
            w_rs.at[arr, source, turn(y, k, ny) if arr == 0 else 0],
            fsdp=turn(y, j, ny) * nx + (x if j else turn(x, i, nx)),
        ).wait_recv()

    def send_along_y(i, stage):
        for j in range(1, ny):
            if stage == ny - j:
                await_shard(1, i, 0, 0)
                along_y(1, i, j, 0).start()
            k = (j + stage) % ny
            await_shard(0, i, 0, k)
            along_y(0, i, j, k).start()

    experts_all = groups * local
    id_f = ids[...].astype(F32)
    gate = gates[...].T
    expert_iota = lax.broadcasted_iota(jnp.int32, (experts_all, rows), 0).astype(F32)
    hit = [(id_f[k:k + 1] == expert_iota).astype(F32) for k in range(2)]
    above = (
        lax.broadcasted_iota(jnp.int32, (rows, rows), 0)
        < lax.broadcasted_iota(jnp.int32, (rows, rows), 1)
    ).astype(F32).astype(BF)
    before = dot((hit[0] + hit[1]).astype(BF), above, 1, 0)
    slot_iota = lax.broadcasted_iota(jnp.int32, (slots, rows), 0).astype(F32)
    cot = cotangent[...].astype(F32)
    grads_slot = None
    for k in range(2):
        slot = jnp.sum(hit[k] * before, axis=0, keepdims=True)
        pick = (id_f[k:k + 1] * cap + slot == slot_iota).astype(F32).astype(BF)
        picks[k] = pick
        descent = (-gate[:, k:k + 1] * cot).astype(BF)
        term = dot(pick, descent, 1, 0)
        grads_slot = term if grads_slot is None else grads_slot + term
    shape = (groups, local, cap, feature)
    tok_send[:, :, 1] = grads_slot.astype(BF).reshape(shape)
    knots_slot = dot(picks[0] + picks[1], states[...], 1, 0)
    tok_send[:, :, 0] = knots_slot.astype(BF).reshape(shape)

    def tok_copy(d, o):
        other, e = turn(g, o, groups), turn(mine, d, local)
        return push(
            tok_send.at[other, e], tok_recv.at[mine, g], tok_ss.at[other, e], tok_rs.at[mine, g],
            expert=other, fsdp=y * nx + q * local + e,
        )

    def tok_arrival(d, o):
        other, e = turn(g, o, groups), turn(mine, d, local)
        return push(
            tok_send.at[other, e], tok_recv.at[e, other], tok_ss.at[other, e], tok_rs.at[e, other],
            expert=other, fsdp=y * nx + q * local + e,
        )

    pl.semaphore_wait(barrier, groups * local - 1 + nx - local + ny - 1)

    over_groups(1, lambda o: tok_copy(0, o).start())
    for i in range(1, nx):
        along_x(1, i, 0).start()
    send_along_y(0, 1)
    for k in range(ny):
        for i in range(1, nx):
            along_x(0, i, k).start()
    for d in range(1, local):
        over_groups(0, lambda o: tok_copy(d, o).start())
    tok_recv[mine, g] = tok_send[g, mine]
    for arr in range(2):
        fulls[arr][f] = shards[arr][mine]

    for i in range(1, nx):
        send_along_y(i, 1)
    for stage in range(2, ny + 1):
        for i in range(nx):
            send_along_y(i, stage)
    over_peers(lambda d, o: tok_arrival(d, o).wait_recv())

    width = max(256, hrows)
    per = width // hrows
    steps = span // width

    def one_copy(arr, j, i, row):
        there, column = turn(y, j, ny), turn(x, i, nx)
        shard = there * nx + column
        if arr == 1:
            return push(
                part_out.at[shard], first_out.at[y, column],
                one_ss.at[1, there, column, 0], one_rs.at[1, y, column, 0],
                fsdp=there * nx + x,
            )
        place = pl.ds(pl.multiple_of(row * span, span), span)
        return push(
            part_in.at[shard, :, place], first_in.at[y, column, :, place],
            one_ss.at[0, there, column, row], one_rs.at[0, y, column, row],
            fsdp=there * nx + x,
        )

    def one_arrival(arr, j, i, row):
        there, column = turn(y, j, ny), turn(x, i, nx)
        shard = there * nx + column
        if arr == 1:
            return push(
                part_out.at[shard], first_out.at[there, column],
                one_ss.at[1, there, column, 0], one_rs.at[1, there, column, 0],
                fsdp=there * nx + x,
            )
        place = pl.ds(pl.multiple_of(row * span, span), span)
        return push(
            part_in.at[shard, :, place], first_in.at[there, column, :, place],
            one_ss.at[0, there, column, row], one_rs.at[0, there, column, row],
            fsdp=there * nx + x,
        )

    knots_t[...] = tok_recv[:, :, 0].reshape(lines, feature).T
    acc_v[...] = jnp.zeros_like(acc_v)
    acc_r[...] = jnp.zeros_like(acc_r)
    for stage in range(1, ny + 1):
        row = turn(y, stage, ny)
        for i in range(nx):
            await_shard(1, i, stage % ny, 0)
            for j in range(ny):
                await_shard(0, i, j, stage % ny)

        def chunk(c, carry):
            knots = tok_recv[:, :, 0].reshape(lines, feature)
            grads = tok_recv[:, :, 1].reshape(lines, feature)
            at = row * steps + c
            columns = pl.ds(pl.multiple_of(at * width, width), width)
            wi = full_in[:, :, columns].reshape(feature, width)
            wo = full_out[pl.ds(at * per, per)].reshape(width, feature)
            preact = dot(knots, wi, 1, 0)
            slope = dot(grads, wo, 1, 1)
            sigma = jax.nn.sigmoid(preact)
            hidden = (preact * sigma).astype(BF)
            inner = (slope * (sigma * (1.0 + preact * (1.0 - sigma)))).astype(BF)
            part_in[:, :, columns] = dot(knots_t[...], inner, 1, 0).astype(BF).reshape(
                fsdp, feature // fsdp, width
            )
            part_out[pl.ds(at * per, per)] = dot(hidden, grads, 0, 0).astype(BF).reshape(
                per, hrows, feature
            )
            acc_v[...] += dot(hidden, wo, 1, 0)
            acc_r[...] += dot(inner, wi, 1, 1)
            return carry

        lax.fori_loop(0, steps, chunk, 0)
        for i in range(1, nx):
            if stage < ny:
                one_copy(1, stage, i, 0).start()
            for j in range(1, ny):
                one_copy(0, j, i, row).start()

    for stage in range(1, ny + 1):
        for j in range(1, ny):
            one_copy(0, j, 0, turn(y, stage, ny)).start()
    for j in range(1, ny):
        one_copy(1, j, 0, 0).start()

    back = (local, groups, cap, feature)
    ret_send[:, :, 0] = acc_v[...].astype(BF).reshape(back)
    ret_send[:, :, 1] = acc_r[...].astype(BF).reshape(back)

    def ret_copy(d, o):
        other, c = turn(g, o, groups), turn(mine, d, local)
        return push(
            ret_send.at[c, other], ret_recv.at[g, mine], ret_ss.at[c, other], ret_rs.at[g, mine],
            expert=other, fsdp=y * nx + q * local + c,
        )

    def ret_arrival(d, o):
        other, c = turn(g, o, groups), turn(mine, d, local)
        return push(
            ret_send.at[c, other], ret_recv.at[other, c], ret_ss.at[c, other], ret_rs.at[other, c],
            expert=other, fsdp=y * nx + q * local + c,
        )

    over_peers(lambda d, o: ret_copy(d, o).start(), -1)
    ret_recv[g, mine] = ret_send[mine, g]

    def two_copy(arr, i, k):
        to = turn(x, i, nx)
        src, dst = sums[arr].at[to], seconds[arr].at[x]
        if arr == 0:
            src, dst = src.at[:, span_at(k)], dst.at[:, span_at(k)]
        return push(
            src, dst, two_ss.at[arr, to, k], two_rs.at[arr, x, k], fsdp=y * nx + to,
        )

    def two_arrival(arr, source):
        for k in range(ny if arr == 0 else 1):
            piece = seconds[arr].at[source]
            if arr == 0:
                piece = piece.at[:, span_at(k)]
            push(
                piece, piece, two_ss.at[arr, source, k], two_rs.at[arr, source, k],
                fsdp=y * nx + source,
            ).wait_recv()

    def summed(arr, i, k):
        column = turn(x, i, nx)
        place = span_at(k) if arr == 0 else slice(None)
        total = parts[arr][y * nx + column, :, place].astype(F32)
        for j in range(1, ny):
            one_arrival(arr, j, i, turn(y, k, ny)).wait_recv()
            total = total + firsts[arr][turn(y, j, ny), column, :, place].astype(F32)
        return total

    for arr, k in [(1, 0)] + [(0, k) for k in range(ny)]:
        place = span_at(k) if arr == 0 else slice(None)
        for i in range(1, nx):
            sums[arr][turn(x, i, nx), :, place] = summed(arr, i, k).astype(BF)
            two_copy(arr, i, k).start()
    for arr, k in [(0, k) for k in range(ny)] + [(1, 0)]:
        place = span_at(k) if arr == 0 else slice(None)
        total = summed(arr, 0, k)
        for other in range(1, sets):
            source = turn(q, other, sets) * local + mine
            if k == 0:
                two_arrival(arr, source)
            total = total + seconds[arr][source, :, place].astype(F32)
        outs[arr][mine, :, place] = total.astype(BF)

    over_peers(lambda d, o: ret_arrival(d, o).wait_recv())
    values = ret_recv[:, :, 0].reshape(slots, feature)
    combined = None
    for k in range(2):
        term = gate[:, k:k + 1] * dot(picks[k], values, 0, 0)
        combined = term if combined is None else combined + term
    defect[...] = (rates[...].astype(F32) - combined).astype(BF)
    returned = ret_recv[:, :, 1].reshape(slots, feature)
    grad_states[...] = dot(picks[0] + picks[1], returned, 0, 0).astype(BF)

    for d in range(1, local):
        e = turn(mine, d, local)
        for arr in (1, 0):
            total = None
            for k in range(sets):
                source = turn(q, k, sets) * local + e
                two_arrival(arr, source)
                term = seconds[arr][source].astype(F32)
                total = term if total is None else total + term
            outs[arr][e] = total.astype(BF)

    over_peers(lambda d, o: tok_copy(d, o).wait_send())
    over_peers(lambda d, o: ret_copy(d, o).wait_send())
    for arr in range(2):
        for i in range(1, nx):
            for k in range(ny if arr == 0 else 1):
                along_x(arr, i, k).wait_send()
                two_copy(arr, i, k).wait_send()
        for j in range(1, ny):
            for i in range(nx):
                for k in range(ny if arr == 0 else 1):
                    along_y(arr, i, j, k).wait_send()
                for row in range(ny if arr == 0 else 1):
                    one_copy(arr, j, i, row).wait_send()


def on_device(states, rates, expert_ids, gate_weights, cotangent, weight_in, weight_out):
    groups, fsdp = lax.axis_size("expert"), lax.axis_size("fsdp")
    rows, feature = states.shape
    drows, local, hidden = weight_in.shape
    hrows = weight_out.shape[0]
    capacity = max(2, 4 * rows // (local * groups))
    cap = -(-capacity // 16) * 16
    nx = math.isqrt(fsdp)
    ny = fsdp // nx
    slots = groups * local * cap
    w_in = jnp.transpose(weight_in, (1, 0, 2))
    w_out = jnp.transpose(weight_out, (1, 0, 2))
    shard_in, shard_out = (drows, hidden), (hrows, feature)
    exchange = (groups, local, 2, cap, feature)
    swapped = (local, groups, 2, cap, feature)
    vmem = pl.BlockSpec(memory_space=pltpu.VMEM)
    dma = pltpu.SemaphoreType.DMA
    defect, grad_states, grad_in, grad_out = pl.pallas_call(
        functools.partial(kernel, (groups, fsdp, nx, ny, local, cap)),
        out_shape=(
            jax.ShapeDtypeStruct((rows, feature), BF),
            jax.ShapeDtypeStruct((rows, feature), BF),
            jax.ShapeDtypeStruct((local,) + shard_in, BF),
            jax.ShapeDtypeStruct((local,) + shard_out, BF),
        ),
        in_specs=[vmem] * 7,
        out_specs=(vmem,) * 4,
        scratch_shapes=[
            pltpu.VMEM(exchange, BF),
            pltpu.VMEM(swapped, BF),
            pltpu.VMEM(swapped, BF),
            pltpu.VMEM(exchange, BF),
            pltpu.VMEM((fsdp,) + shard_in, BF),
            pltpu.VMEM((fsdp,) + shard_out, BF),
            pltpu.VMEM((fsdp,) + shard_in, BF),
            pltpu.VMEM((fsdp,) + shard_out, BF),
            pltpu.VMEM((ny, nx) + shard_in, BF),
            pltpu.VMEM((ny, nx) + shard_out, BF),
            pltpu.VMEM((nx,) + shard_in, BF),
            pltpu.VMEM((nx,) + shard_out, BF),
            pltpu.VMEM((nx,) + shard_in, BF),
            pltpu.VMEM((nx,) + shard_out, BF),
            pltpu.VMEM((local * groups * cap, feature), F32),
            pltpu.VMEM((local * groups * cap, feature), F32),
            pltpu.VMEM((2, slots, rows), BF),
            pltpu.VMEM((feature, local * groups * cap), BF),
            dma((groups, local)),
            dma((local, groups)),
            dma((local, groups)),
            dma((groups, local)),
            dma((2, nx, ny, ny)),
            dma((2, fsdp, ny)),
            dma((2, ny, nx, ny)),
            dma((2, ny, nx, ny)),
            dma((2, nx, ny)),
            dma((2, nx, ny)),
        ],
        compiler_params=pltpu.CompilerParams(
            collective_id=0, has_side_effects=True, vmem_limit_bytes=36 * 1024 * 1024
        ),
    )(states, rates, expert_ids.T, gate_weights.T, cotangent, w_in, w_out)
    return (
        defect,
        grad_states,
        jnp.transpose(grad_in, (1, 0, 2)),
        jnp.transpose(grad_out, (1, 0, 2)),
    )


def solution(mesh):
    placed = (
        P(("expert", "fsdp"), None),
        P(("expert", "fsdp"), None),
        P(("expert", "fsdp"), None),
        P(("expert", "fsdp"), None),
        P(("expert", "fsdp"), None),
        P("fsdp", "expert", None),
        P("fsdp", "expert", None),
    )
    return jax.shard_map(
        on_device,
        mesh=mesh,
        in_specs=placed,
        out_specs=(
            P(("expert", "fsdp"), None),
            P(("expert", "fsdp"), None),
            P("fsdp", "expert", None),
            P("fsdp", "expert", None),
        ),
        check_vma=False,
    )
```
